32 devices in a mesh: dp: 4 (over x, core), fsdp: 8 (over z, y).
Axes of the slice: x: 2, y: 2, z: 4, core: 2. Of those that a mesh axis runs over, the one named last changes fastest.
Arguments:
- tokens: bfloat16 [32768, 1024], P(('dp', 'fsdp')), may hold values from -6 to 6
- doc_lengths: int32 [32, 8], P(('dp', 'fsdp')), may hold values from 0 to 1024, as said below
- gain_one: bfloat16 [1024], P(('dp', 'fsdp')), may hold values from 0.099609375 to 1.8984375
- query_weight: bfloat16 [1024, 1024], P(('dp', 'fsdp')), may hold values from -0.1875 to 0.1875
- key_weight: bfloat16 [1024, 128], P(('dp', 'fsdp')), may hold values from -0.1875 to 0.1875
- value_weight: bfloat16 [1024, 128], P(('dp', 'fsdp')), may hold values from -0.1875 to 0.1875
- out_weight: bfloat16 [1024, 1024], P(('dp', 'fsdp')), may hold values from -0.75 to 0.75
- gain_two: bfloat16 [1024], P(('dp', 'fsdp')), may hold values from 0.099609375 to 1.8984375
- up_weight: bfloat16 [1024, 4096], P(('dp', 'fsdp')), may hold values from -0.1875 to 0.1875
- down_weight: bfloat16 [4096, 1024], P(('dp', 'fsdp')), may hold values from -0.09375 to 0.09375
- cotangent: bfloat16 [32768, 1024], P(('dp', 'fsdp')), may hold values from -6 to 6
Outputs:
- output: bfloat16 [32768, 1024], P(('dp', 'fsdp'))
- grad_tokens: bfloat16 [32768, 1024], P(('dp', 'fsdp'))
- grad_gain_one: float32 [1024], P(('dp', 'fsdp'))
- grad_query_weight: float32 [1024, 1024], P(('dp', 'fsdp'))
- grad_key_weight: float32 [1024, 128], P(('dp', 'fsdp'))
- grad_value_weight: float32 [1024, 128], P(('dp', 'fsdp'))
- grad_out_weight: float32 [1024, 1024], P(('dp', 'fsdp'))
- grad_gain_two: float32 [1024], P(('dp', 'fsdp'))
- grad_up_weight: float32 [1024, 4096], P(('dp', 'fsdp'))
- grad_down_weight: float32 [4096, 1024], P(('dp', 'fsdp'))
The draws below stay inside these ranges and needn't reach their ends.
Inputs may be any that keep to these rules, and one draw needn't show every extreme that they name: `doc_lengths`: row d belongs to device d along dp+fsdp (dp outer). Each row sums to at most 1024; a zero length is an empty slot. In every draw one device holds a single sequence of 1024 tokens.
All inputs are finite; a program needn't handle non-finite values.
Results may differ from the reference program's by a relative error of at most 0.012.
Values may be sent and summed in bfloat16 or wider, within the bound.
No kernel may reach another device: no remote copies, remote signals or barrier semaphores. Data moves between devices by JAX's collectives and lax.ppermute only.
A program may use at most 256 MiB of HBM per device.

```python
import math
import jax
import jax.numpy as jnp
from jax import lax

D = 1024
HEADS = 8
HEAD = 128
FF = 4096
TOK_DEV = 1024
SLOTS = 8
TOKENS = 32768
DEVICES = 32


def draw_doc_lengths(key, part):
    key = jax.random.fold_in(key, 11)
    key_expo, key_pad, key_full = jax.random.split(key, 3)
    exponent = jax.random.randint(key_expo, (DEVICES, SLOTS), 0, 7)
    shares = jnp.left_shift(jnp.ones((DEVICES, SLOTS), jnp.int32), exponent.astype(jnp.int32))
    padding = jax.random.randint(key_pad, (DEVICES, 1), 0, TOK_DEV // 8 + 1)
    usable = TOK_DEV - padding
    share_total = jnp.sum(shares, axis=1, keepdims=True)
    lengths = shares * usable // share_total
    full_row = jax.random.randint(key_full, (), 0, DEVICES)
    single = jnp.where(jnp.arange(SLOTS)[None, :] == 0, TOK_DEV, 0) * jnp.ones((DEVICES, 1), jnp.int32)
    chosen = jnp.arange(DEVICES)[:, None] == full_row
    return jnp.where(chosen, single, lengths).astype(jnp.int32)


def block_levels(stream_key, extent, pieces, low, top_value):
    level = 1.0
    for dim, blocks in pieces:
        steps = jax.random.uniform(jax.random.fold_in(jax.random.fold_in(stream_key, 6), dim), (blocks,), jnp.float32, low / len(pieces), top_value / len(pieces))
        level = level * jnp.repeat(jnp.exp(steps), extent[dim] // blocks).reshape((-1,) + (1,) * (len(extent) - 1 - dim))
    return level


def scatter_about(stream_key, dims, deviation, limit, cuts=(), kind=jnp.bfloat16):
    array = jax.random.normal(stream_key, dims, jnp.float32) * deviation
    if len(cuts) > 0:
        array = block_levels(stream_key, dims, cuts, -0.22, 0.18) * array
    return jnp.clip(array, min=-limit, max=limit).astype(kind)


def setup_inputs(seed: int = 0) -> dict:
    key_list = jax.random.split(jax.random.key(seed), 12)
    return {
        "tokens": scatter_about(key_list[0], (TOKENS, D), 1.0, 6.0, ((0, 32),)),
        "doc_lengths": draw_doc_lengths(jax.random.fold_in(key_list[11], 71), 0),
        "gain_one": jnp.clip(1.0 + 0.18 * jax.random.normal(key_list[2], (D,), jnp.float32), 0.099609375, 1.8984375).astype(jnp.bfloat16),
        "query_weight": scatter_about(key_list[3], (D, HEADS * HEAD), D ** -0.5, 0.1875, ((0, 32),)),
        "key_weight": scatter_about(key_list[4], (D, HEAD), D ** -0.5, 0.1875, ((0, 32),)),
        "value_weight": scatter_about(key_list[5], (D, HEAD), D ** -0.5, 0.1875, ((0, 32),)),
        "out_weight": scatter_about(key_list[6], (HEADS * HEAD, D), (HEADS * HEAD // 16) ** -0.5, 0.75, ((0, 32),)),
        "gain_two": jnp.clip(1.0 + 0.18 * jax.random.normal(key_list[7], (D,), jnp.float32), 0.099609375, 1.8984375).astype(jnp.bfloat16),
        "up_weight": scatter_about(key_list[8], (D, FF), D ** -0.5, 0.1875, ((0, 32),)),
        "down_weight": scatter_about(key_list[9], (FF, D), FF ** -0.5, 0.09375, ((0, 32),)),
        "cotangent": scatter_about(key_list[10], (TOKENS, D), 1.0, 6.0, ((0, 32),)),
    }


epsilon = 1e-06
highest = lax.Precision.HIGHEST

@jax.custom_vjp
def low(v):
    return lax.optimization_barrier(v.astype(jnp.bfloat16)).astype(jnp.float32)

@jax.custom_vjp
def low_back(v):
    return v

def low_keep(v):
    return (low(v), None)

def low_pass(kept, grad):
    return (grad,)

def back_keep(v):
    return (v, None)

def back_low(kept, grad):
    return (low(grad),)
low.defvjp(low_keep, low_pass)
low_back.defvjp(back_keep, back_low)

def pack_mask(lengths, row_count):
    position = jnp.arange(row_count, dtype=jnp.int32)
    seq_ends = jnp.cumsum(lengths.astype(jnp.int32)).astype(jnp.int32)
    segment = lax.optimization_barrier(jnp.sum((position[:, None] >= seq_ends[None, :]).astype(jnp.int32), axis=1))
    padding = position >= seq_ends[-1]
    causal = position[None, :] <= position[:, None]
    allowed = (segment[:, None] == segment[None, :]) & causal & jnp.logical_not(padding)[None, :]
    return allowed | (position[:, None] == position[None, :])

def norm_rows(inputs, gain):
    return inputs * lax.rsqrt(lax.optimization_barrier(jnp.mean(inputs * inputs, axis=-1, keepdims=True)) + epsilon) * gain

def layer_forward(params, token_rows, lengths):
    gain_one, query_weight, key_weight, value_weight, out_weight, gain_two, up_weight, down_weight = params
    row_count = token_rows.shape[0]
    allowed = pack_mask(lengths, row_count)
    normed = low(norm_rows(token_rows, gain_one))
    queries = low_back(low(jnp.dot(normed, query_weight, precision=highest)))
    key_rows = low_back(low(jnp.dot(normed, key_weight, precision=highest)))
    value_rows = low_back(low(jnp.dot(normed, value_weight, precision=highest)))
    query_heads = queries.reshape(row_count, HEADS, HEAD)
    scores = low_back(jnp.einsum('qhe,ke->hqk', query_heads, key_rows, precision=highest) * (1.0 / math.sqrt(HEAD)))
    scores = jnp.where(allowed[None], scores, -1e+30)
    row_peak = lax.optimization_barrier(jnp.max(scores, axis=-1, keepdims=True))
    exponent = jnp.exp(scores - row_peak)
    probabilities = exponent / lax.optimization_barrier(jnp.sum(exponent, axis=-1, keepdims=True))
    attended = jnp.einsum('hqk,ke->qhe', low(probabilities), value_rows, precision=highest)
    attended = low_back(low(attended.reshape(row_count, HEADS * HEAD)))
    hidden = token_rows + low_back(jnp.dot(attended, out_weight, precision=highest))
    normed_two = low(norm_rows(hidden, gain_two))
    inner = low_back(jnp.dot(normed_two, up_weight, precision=highest))
    active = low(jax.nn.gelu(inner))
    return hidden + low_back(jnp.dot(active, down_weight, precision=highest))

def reference(tokens, doc_lengths, gain_one, query_weight, key_weight, value_weight, out_weight, gain_two, up_weight, down_weight, cotangent):
    params = (gain_one.astype(jnp.float32), query_weight.astype(jnp.float32), key_weight.astype(jnp.float32), value_weight.astype(jnp.float32), out_weight.astype(jnp.float32), gain_two.astype(jnp.float32), up_weight.astype(jnp.float32), down_weight.astype(jnp.float32))
    pack_count = tokens.shape[0] // TOK_DEV
    token_packs = tokens.astype(jnp.float32).reshape(pack_count, TOK_DEV, D)

    def forward(pack_rows, weight_set):

        def one_pack(scan_carry, pack_item):
            return (scan_carry, jax.checkpoint(layer_forward)(weight_set, pack_item[0], pack_item[1]))
        unused, outputs = lax.scan(one_pack, jnp.int32(0), (pack_rows, doc_lengths))
        return outputs
    outputs, pullback = jax.vjp(forward, token_packs, params)
    grad_packs, grad_params = pullback(cotangent.astype(jnp.float32).reshape(pack_count, TOK_DEV, D))
    return (outputs.reshape(TOKENS, D).astype(jnp.bfloat16), grad_packs.reshape(TOKENS, D).astype(jnp.bfloat16), grad_params[0].astype(jnp.float32), grad_params[1].astype(jnp.float32), grad_params[2].astype(jnp.float32), grad_params[3].astype(jnp.float32), grad_params[4].astype(jnp.float32), grad_params[5].astype(jnp.float32), grad_params[6].astype(jnp.float32), grad_params[7].astype(jnp.float32))
```

```python
import functools
import math

import jax
import jax.numpy as jnp
from jax import lax
from jax.experimental import pallas as pl
from jax.experimental.pallas import tpu as pltpu
from jax.sharding import Mesh, PartitionSpec as P

EPS = 1e-06
HEAD = 128
MIB = 2**20
f32 = jnp.float32
bf16 = jnp.bfloat16
VM = pl.BlockSpec(memory_space=pltpu.VMEM)
SM = pl.BlockSpec(memory_space=pltpu.SMEM)
GELU_A = math.sqrt(2.0 / math.pi)
GELU_B = GELU_A * 0.044715
SCORE_SCALE = 1.0 / math.sqrt(HEAD)
LOG2E = math.log2(math.e)


def nn(a, b):
    return lax.dot_general(a, b, (((1,), (0,)), ((), ())), preferred_element_type=f32)


def nt(a, b):
    return lax.dot_general(a, b, (((1,), (1,)), ((), ())), preferred_element_type=f32)


def tn(a, b):
    return lax.dot_general(a, b, (((0,), (0,)), ((), ())), preferred_element_type=f32)


def shape(dims, dtype):
    return jax.ShapeDtypeStruct(dims, dtype)


def call(kernel, outs, args, flops, exps=0, scratch=(), vmem=48, name=None, in_specs=None, **kw):
    moved = sum(math.prod(a.shape) * a.dtype.itemsize for a in (*args, *outs))
    return pl.pallas_call(
        kernel,
        out_shape=outs,
        in_specs=in_specs or [VM] * len(args),
        out_specs=kw.pop("out_specs", [VM] * len(outs)),
        scratch_shapes=list(scratch),
        compiler_params=pltpu.CompilerParams(vmem_limit_bytes=vmem * MIB),
        cost_estimate=pl.CostEstimate(flops=flops, bytes_accessed=moved, transcendentals=exps),
        name=name,
        **kw,
    )(*args)


def mask_bias(len_ref, first, rows, cols):
    q_pos = first + lax.broadcasted_iota(jnp.int32, (rows, 1), 0)
    k_pos = lax.broadcasted_iota(jnp.int32, (1, cols), 1)
    q_seg = jnp.zeros((rows, 1), jnp.int32)
    k_seg = jnp.zeros((1, cols), jnp.int32)
    end = jnp.int32(0)
    for slot in range(len_ref.shape[1]):
        end = end + len_ref[0, slot]
        q_seg = q_seg + (q_pos >= end).astype(jnp.int32)
        k_seg = k_seg + (k_pos >= end).astype(jnp.int32)
    k_seg = jnp.where(k_pos >= end, -1, k_seg)
    allowed = ((q_seg == k_seg) & (k_pos <= q_pos)) | (k_pos == q_pos)
    return jnp.where(allowed, 0.0, -1e30).astype(f32)


def gain_rows(block):
    return block.astype(f32).T


def norm_tile(x, gain):
    r = lax.rsqrt(jnp.mean(x * x, axis=-1, keepdims=True) + EPS)
    return x * r * gain


def attention_forward_kernel(len_ref, x_ref, w_ref, qkv_ref, att_ref, gains, normed, bias):
    rows, model = x_ref.shape
    wide = qkv_ref.shape[1]
    heads = (wide - 2 * HEAD) // HEAD
    gains[...] = gain_rows(w_ref[:, wide : wide + HEAD])[:8]

    @pl.loop(0, rows // 128)
    def _(t):
        at = pl.ds(pl.multiple_of(t * 128, 128), 128)
        normed[at, :] = norm_tile(x_ref[at, :].astype(f32), gains[0:1, :]).astype(bf16)

    @pl.loop(0, wide // 256)
    def _(j):
        at = pl.ds(pl.multiple_of(j * 256, 256), 256)
        qkv_ref[:, at] = nn(normed[...], w_ref[:, at]).astype(bf16)

    key_at = heads * HEAD
    for i in range(rows // 128):
        ext = (i + 1) * 128
        q_at = slice(i * 128, ext)
        bias[:, :ext] = mask_bias(len_ref, i * 128, 128, ext)

        @pl.loop(0, heads // 2)
        def _(pair):
            at = pl.ds(pl.multiple_of(pair * 256, 256), 256)
            both = qkv_ref[q_at, at]
            q = jnp.concatenate([both[:, :HEAD], both[:, HEAD:]], axis=0)
            s = nt(q, qkv_ref[:ext, key_at : key_at + HEAD]) * (SCORE_SCALE * LOG2E)
            s = s.reshape(2, 128, ext) + bias[:, :ext][None]
            s = s.reshape(256, ext)
            e = jnp.exp2(s - jnp.max(s, axis=-1, keepdims=True))
            p = e * (1.0 / jnp.sum(e, axis=-1, keepdims=True))
            o = nn(p.astype(bf16), qkv_ref[:ext, key_at + HEAD :]).astype(bf16)
            att_ref[q_at, at] = jnp.concatenate([o[:128], o[128:]], axis=1)


def attention_forward(lengths, x, w):
    rows, model = x.shape
    wide = w.shape[1] - HEAD
    return call(
        attention_forward_kernel,
        [shape((rows, wide), bf16), shape((rows, wide - 2 * HEAD), bf16)],
        (lengths, x, w),
        2 * rows * model * wide + 4 * rows * rows * model,
        rows * rows * 4,
        [pltpu.VMEM((8, model), f32), pltpu.VMEM((rows, model), bf16), pltpu.VMEM((128, rows), f32)],
        40,
        "attention_forward",
        [SM, VM, VM],
    )


def branch_kernel(x_ref, att_ref, wo_ref, w_ref, hidden_ref, nt_ref, gains):
    rows = x_ref.shape[0]
    gains[...] = gain_rows(w_ref[...])[:8]
    model = wo_ref.shape[1]

    @pl.loop(0, model // 256)
    def _(j):
        at = pl.ds(pl.multiple_of(j * 256, 256), 256)
        hidden_ref[:, at] = x_ref[:, at].astype(f32) + nn(att_ref[...], wo_ref[:, at])

    @pl.loop(0, rows // 128)
    def _(t):
        at = pl.ds(pl.multiple_of(t * 128, 128), 128)
        nt_ref[at, :] = norm_tile(hidden_ref[at, :], gains[1:2, :]).astype(bf16)


def branch(x, att, wo, w):
    rows, model = x.shape
    last = w.shape[1] // HEAD - 1
    whole = lambda a: pl.BlockSpec(a.shape, lambda i: (0, 0))
    return call(
        branch_kernel,
        [shape((rows, model), f32), shape((rows, model), bf16)],
        (x, att, wo, w),
        2 * rows * model * model,
        0,
        [pltpu.VMEM((8, model), f32)],
        40,
        "branch",
        [whole(x), whole(att), whole(wo), pl.BlockSpec((model, HEAD), lambda i: (0, last))],
        grid=(1,),
        out_specs=[whole(x), whole(x)],
    )


def gelu_both(v):
    v2 = v * v
    t = jnp.tanh(v * (GELU_A + GELU_B * v2))
    h = 0.5 + 0.5 * t
    a = v * h
    return a, h + (a - a * h) * ((2 * GELU_A) + (6 * GELU_B) * v2)


def ffn_kernel(groups, nt_o, nt_p, dy_o, dy_p, g_ref, act_o, act_p, gi_o, gi_p, gg_ref, us):
    model = nt_o.shape[1]
    part = g_ref.shape[1] // 4
    rows = model // groups
    for g in range(groups):
        us[g * rows : (g + 1) * rows, :] = g_ref[
            (g // 2) * rows : (g // 2 + 1) * rows, (g % 2) * part : (g % 2 + 1) * part
        ]
    tile = min(256, part)
    for j in range(part // tile):
        cols = slice(j * tile, (j + 1) * tile)
        for n_ref, y_ref, a_ref, i_ref in ((nt_o, dy_o, act_o, gi_o), (nt_p, dy_p, act_p, gi_p)):
            inner = nn(n_ref[...], us[:, cols])
            ga = nt(y_ref[...], g_ref[cols, 2 * part :])
            a, slope = gelu_both(inner)
            a_ref[:, cols] = a.astype(bf16)
            i_ref[:, cols] = (ga * slope).astype(bf16)
        v = (tn(nt_o[...], gi_o[:, cols]) + tn(nt_p[...], gi_p[:, cols])).astype(bf16)
        for g in range(groups):
            gg_ref[
                (g // 2) * rows : (g // 2 + 1) * rows,
                (g % 2) * part + j * tile : (g % 2) * part + (j + 1) * tile,
            ] = v[g * rows : (g + 1) * rows]
        v = tn(act_o[:, cols], dy_o[...]) + tn(act_p[:, cols], dy_p[...])
        gg_ref[cols, 2 * part :] = v.astype(bf16)


def ffn(groups, nt_o, nt_p, dy_o, dy_p, g):
    rows, model = nt_o.shape
    steps = g.shape[1] // (2 * model)
    part = model // 2
    once = pl.BlockSpec((rows, model), lambda c: (0, 0), pipeline_mode=pl.Buffered(1))
    piece = pl.BlockSpec((part, 2 * model), lambda c: (0, c))
    seen = pl.BlockSpec((rows, part), lambda c: (0, c))
    return call(
        functools.partial(ffn_kernel, groups),
        [shape((rows, steps * part), bf16)] * 4 + [shape(g.shape, bf16)],
        (nt_o, nt_p, dy_o, dy_p, g),
        steps * 16 * rows * model * part,
        steps * 2 * rows * part,
        [pltpu.VMEM((model, part), bf16)],
        48,
        "ffn",
        [once] * 4 + [piece],
        grid=(steps,),
        out_specs=[seen] * 4 + [piece],
    )


def ffn_sum_kernel(count, *refs):
    acts, gis = refs[:count], refs[count : 2 * count]
    downs, ups = refs[2 * count : 3 * count], refs[3 * count : 4 * count]
    out_ref, gn_ref = refs[4 * count :]
    out = gn = None
    for a, i, d, u in zip(acts, gis, downs, ups):
        o = nn(a[...], d[...])
        n = nt(i[...], u[...])
        out = o if out is None else out + o
        gn = n if gn is None else gn + n
    out_ref[...] = out.astype(bf16)
    gn_ref[...] = gn.astype(bf16)


def ffn_sum(groups, acts, gis, gathered):
    rows, part = acts[0][0].shape[0], gathered[0][0].shape[0]
    model = 2 * part
    count = len(acts)
    wide = model // groups
    a_specs = [pl.BlockSpec((rows, part), lambda g, c=c: (0, c), pipeline_mode=pl.Buffered(1)) for _, c in acts]
    d_specs = [pl.BlockSpec((part, wide), lambda g, c=c: (0, (c * 2 + 1) * groups + g)) for _, c in gathered]
    u_specs = [pl.BlockSpec((wide, part), lambda g, c=c: (g // 2, c * 4 + g % 2)) for _, c in gathered]
    out = pl.BlockSpec((rows, wide), lambda g: (0, g))
    return call(
        functools.partial(ffn_sum_kernel, count),
        [shape((rows, model), bf16)] * 2,
        (*[a for a, _ in acts], *[a for a, _ in gis], *[a for a, _ in gathered], *[a for a, _ in gathered]),
        count * 4 * rows * part * model,
        0,
        (),
        48,
        "ffn_sum",
        a_specs * 2 + d_specs + u_specs,
        grid=(groups,),
        out_specs=[out, out],
    )


def branch_backward_kernel(
    hidden_ref, gn_o, gn_p, out_o, out_p, dy_ref, wo_ref, w_ref, att_ref,
    output_ref, gh_ref, gatt_ref, gwo_ref, gg_ref, gains, gb,
):
    rows, model = hidden_ref.shape
    gains[...] = gain_rows(w_ref[...])[:8]
    gg_ref[...] = jnp.zeros_like(gg_ref)

    @pl.loop(0, rows // 64)
    def _(t):
        at = pl.ds(pl.multiple_of(t * 64, 64), 64)
        h = hidden_ref[at, :]
        output_ref[at, :] = (h + (out_o[at, :].astype(f32) + out_p[at, :].astype(f32))).astype(bf16)
        gn = gn_o[at, :].astype(f32) + gn_p[at, :].astype(f32)
        r = lax.rsqrt(jnp.mean(h * h, axis=-1, keepdims=True) + EPS)
        z = h * r
        gg_ref[1:2, :] += jnp.sum(gn * z, axis=0, keepdims=True)
        g = gn * gains[1:2, :]
        gh = dy_ref[at, :].astype(f32) + r * (g - z * jnp.mean(g * z, axis=-1, keepdims=True))
        gh_ref[at, :] = gh
        gb[at, :] = gh.astype(bf16)

    @pl.loop(0, model // 256)
    def _(j):
        at = pl.ds(pl.multiple_of(j * 256, 256), 256)
        gatt_ref[:, at] = nt(gb[...], wo_ref[at, :]).astype(bf16)
        gwo_ref[:, at] = tn(att_ref[...], gb[:, at]).astype(bf16)


def branch_backward(hidden, gn_o, gn_p, out_o, out_p, dy, wo, w, att):
    rows, model = hidden.shape
    last = w.shape[1] // HEAD - 1
    whole = lambda a: pl.BlockSpec(a.shape, lambda i: (0, 0))
    args = (hidden, gn_o, gn_p, out_o, out_p, dy, wo, w, att)
    outs = [
        shape((rows, model), bf16),
        shape((rows, model), f32),
        shape((rows, model), bf16),
        shape(wo.shape, bf16),
        shape((8, model), f32),
    ]
    return call(
        branch_backward_kernel,
        outs,
        args,
        4 * rows * model * model,
        0,
        [pltpu.VMEM((8, model), f32), pltpu.VMEM((rows, model), bf16)],
        56,
        "branch_backward",
        [*map(whole, args[:7]), pl.BlockSpec((model, HEAD), lambda i: (0, last)), whole(att)],
        grid=(1,),
        out_specs=[*map(whole, outs)],
    )


def attention_backward_kernel(len_ref, qkv_ref, ga_ref, g_ref, bias, dk, dv):
    rows, wide = qkv_ref.shape
    heads = (wide - 2 * HEAD) // HEAD
    key_at = heads * HEAD
    dk[...] = jnp.zeros_like(dk)
    dv[...] = jnp.zeros_like(dv)
    for i in range(rows // 128):
        ext = (i + 1) * 128
        q_at = slice(i * 128, ext)
        bias[:, :ext] = mask_bias(len_ref, i * 128, 128, ext)

        @pl.loop(0, heads // 2)
        def _(pair):
            at = pl.ds(pl.multiple_of(pair * 256, 256), 256)
            both = qkv_ref[q_at, at]
            q = jnp.concatenate([both[:, :HEAD], both[:, HEAD:]], axis=0)
            both = ga_ref[q_at, at]
            ga = jnp.concatenate([both[:, :HEAD], both[:, HEAD:]], axis=0)
            keys = qkv_ref[:ext, key_at : key_at + HEAD]
            s = nt(q, keys) * (SCORE_SCALE * LOG2E)
            s = s.reshape(2, 128, ext) + bias[:, :ext][None]
            s = s.reshape(256, ext)
            e = jnp.exp2(s - jnp.max(s, axis=-1, keepdims=True))
            p = e * (1.0 / jnp.sum(e, axis=-1, keepdims=True))
            gp = nt(ga, qkv_ref[:ext, key_at + HEAD :])
            pg = p * gp
            gs = (pg - p * jnp.sum(pg, axis=-1, keepdims=True)).astype(bf16)
            dv[:ext, :] += tn(p.astype(bf16), ga)
            dk[:ext, :] += tn(gs, q)
            gq = (nn(gs, keys) * SCORE_SCALE).astype(bf16)
            g_ref[q_at, at] = jnp.concatenate([gq[:128], gq[128:]], axis=1)

    g_ref[:, key_at : key_at + HEAD] = (dk[...] * SCORE_SCALE).astype(bf16)
    g_ref[:, key_at + HEAD :] = dv[...].astype(bf16)


def attention_backward(lengths, qkv, ga):
    rows, wide = qkv.shape
    model = ga.shape[1]
    return call(
        attention_backward_kernel,
        [shape(qkv.shape, bf16)],
        (lengths, qkv, ga),
        10 * rows * rows * model,
        rows * rows * 4,
        [pltpu.VMEM((128, rows), f32), pltpu.VMEM((rows, HEAD), f32), pltpu.VMEM((rows, HEAD), f32)],
        40,
        "attention_backward",
        [SM, VM, VM],
    )[0]


def input_backward_kernel(x_ref, g_ref, w_ref, gh_ref, gg_ref, gx_ref, gw_ref, gains, normed, gn, sums):
    rows, model = x_ref.shape
    wide = g_ref.shape[1]
    gains[...] = gain_rows(w_ref[:, wide : wide + HEAD])[:8]
    sums[...] = jnp.zeros_like(sums)
    sums[0:8, :] = gg_ref[...]

    @pl.loop(0, rows // 128)
    def _(t):
        at = pl.ds(pl.multiple_of(t * 128, 128), 128)
        normed[at, :] = norm_tile(x_ref[at, :].astype(f32), gains[0:1, :]).astype(bf16)

    @pl.loop(0, model // 256)
    def _(j):
        at = pl.ds(pl.multiple_of(j * 256, 256), 256)
        gn[:, at] = nt(g_ref[...], w_ref[at, :wide])

    @pl.loop(0, wide // 256)
    def _(j):
        at = pl.ds(pl.multiple_of(j * 256, 256), 256)
        gw_ref[:, at] = tn(normed[...], g_ref[:, at]).astype(bf16)

    @pl.loop(0, rows // 64)
    def _(t):
        at = pl.ds(pl.multiple_of(t * 64, 64), 64)
        x = x_ref[at, :].astype(f32)
        n = gn[at, :]
        r = lax.rsqrt(jnp.mean(x * x, axis=-1, keepdims=True) + EPS)
        z = x * r
        sums[0:1, :] += jnp.sum(n * z, axis=0, keepdims=True)
        g = n * gains[0:1, :]
        gx_ref[at, :] = (gh_ref[at, :] + r * (g - z * jnp.mean(g * z, axis=-1, keepdims=True))).astype(bf16)

    gw_ref[:, wide : wide + HEAD] = sums[...].T.astype(bf16)


def input_backward(x, g, w, gh, gg):
    rows, model = x.shape
    wide = g.shape[1]
    return call(
        input_backward_kernel,
        [shape(x.shape, bf16), shape(w.shape, bf16)],
        (x, g, w, gh, gg),
        4 * rows * model * wide,
        0,
        [
            pltpu.VMEM((8, model), f32),
            pltpu.VMEM((rows, model), bf16),
            pltpu.VMEM((rows, model), f32),
            pltpu.VMEM((HEAD, model), f32),
        ],
        56,
        "input_backward",
    )


def on_device(
    sizes, tokens, doc_lengths, gain_one, query_weight, key_weight, value_weight, out_weight,
    gain_two, up_weight, down_weight, cotangent,
):
    chips_x, fsdp = sizes
    every = ("x", "core", "fsdp")
    chips = ("x", "fsdp")
    core = lax.axis_index("core")
    swap = lambda a: lax.ppermute(a, "core", [(0, 1), (1, 0)])
    rows, model = tokens.shape
    shard = query_weight.shape[0]
    ff = up_weight.shape[1]
    chunks = down_weight.shape[0] // shard
    part = ff // (2 * chunks)
    groups = chips_x * 2

    gain_block = jnp.zeros((shard, HEAD), bf16).at[:, 0].set(gain_one).at[:, 1].set(gain_two)
    w_rows = jnp.concatenate([query_weight, key_weight, value_weight, gain_block], axis=1)
    w = lax.all_gather(w_rows, every, axis=0, tiled=True)
    wo = lax.all_gather(out_weight, every, axis=0, tiled=True)

    dy_p = swap(cotangent)
    up = up_weight.reshape(shard, chips_x, 2, fsdp, chunks, shard).transpose(2, 0, 4, 1, 3, 5)
    up = up.reshape(2, shard, chunks, part)
    up_keep = jnp.where(core == 0, up[0], up[1])
    up_come = swap(jnp.where(core == 0, up[1], up[0]))
    up_pair = jnp.where(core == 0, jnp.stack([up_keep, up_come], 2), jnp.stack([up_come, up_keep], 2))
    up_pair = up_pair.reshape(shard, chunks, 2 * part)
    down = down_weight.reshape(chunks, shard, model)
    per_call = 2
    gathered = []
    for first in range(0, chunks, per_call):
        pieces = []
        for c in range(first, first + per_call):
            pieces += [up_pair[:, c], down[c]]
        gathered.append(lax.all_gather(jnp.concatenate(pieces, axis=1), chips, axis=0, tiled=True))

    qkv, att = attention_forward(doc_lengths, tokens, w)
    hidden, nt_o = branch(tokens, att, wo, w)
    nt_p = swap(nt_o)

    acts_o, acts_p, gis_o, gis_p, places, ffn_sums = [], [], [], [], [], []
    for g in gathered:
        act_o, act_p, gi_o, gi_p, grads = ffn(groups, nt_o, nt_p, cotangent, dy_p, g)
        ffn_sums.append(lax.psum_scatter(grads, chips, scatter_dimension=0, tiled=True))
        for c in range(per_call):
            acts_o.append((act_o, c))
            acts_p.append((act_p, c))
            gis_o.append((gi_o, c))
            gis_p.append((gi_p, c))
            places.append((g, c))
    out_p, gn_p = ffn_sum(groups, acts_p, gis_p, places)
    out_r, gn_r = swap(out_p), swap(gn_p)
    out_o, gn_o = ffn_sum(groups, acts_o, gis_o, places)

    output, gh, gatt, gwo, gg = branch_backward(hidden, gn_o, gn_r, out_o, out_r, cotangent, wo, w, att)
    grad_out = lax.psum_scatter(gwo, every, scatter_dimension=0, tiled=True).astype(f32)
    gqkv = attention_backward(doc_lengths, qkv, gatt)
    grad_tokens, gw = input_backward(tokens, gqkv, w, gh, gg)
    gw = lax.psum_scatter(gw, every, scatter_dimension=0, tiled=True).astype(f32)

    sums = jnp.concatenate([s.reshape(shard, per_call, 2 * model) for s in ffn_sums], axis=1)
    grad_down = sums[:, :, model:].transpose(1, 0, 2).reshape(chunks * shard, model).astype(f32)
    g_up = sums[:, :, :model].reshape(shard, chunks, 2, part)
    keep = jnp.where(core == 0, g_up[:, :, 0], g_up[:, :, 1])
    come = swap(jnp.where(core == 0, g_up[:, :, 1], g_up[:, :, 0]))
    grad_up = jnp.where(core == 0, jnp.stack([keep, come], 0), jnp.stack([come, keep], 0))
    grad_up = grad_up.reshape(2, shard, chunks, chips_x, fsdp, shard).transpose(1, 3, 0, 4, 2, 5)
    grad_up = grad_up.reshape(shard, ff).astype(f32)

    qw = query_weight.shape[1]
    return (
        output,
        grad_tokens,
        gw[:, qw + 2 * HEAD],
        gw[:, :qw],
        gw[:, qw : qw + HEAD],
        gw[:, qw + HEAD : qw + 2 * HEAD],
        grad_out,
        gw[:, qw + 2 * HEAD + 1],
        grad_up,
        grad_down,
    )


def solution(mesh):
    dp, fsdp = mesh.shape["dp"], mesh.shape["fsdp"]
    split = Mesh(mesh.devices.reshape(dp // 2, 2, fsdp), ("x", "core", "fsdp"))
    rows = P(("x", "core", "fsdp"), None)
    line = P(("x", "core", "fsdp"))
    return jax.shard_map(
        functools.partial(on_device, (dp // 2, fsdp)),
        mesh=split,
        in_specs=(rows, rows, line, rows, rows, rows, rows, line, rows, rows, rows),
        out_specs=(rows, rows, line, rows, rows, rows, rows, line, rows, rows),
        check_vma=False,
    )
```

```python
import functools
import math

import jax
import jax.numpy as jnp
from jax import lax
from jax.experimental import pallas as pl
from jax.experimental.pallas import tpu as pltpu
from jax.sharding import Mesh, PartitionSpec as P

EPS = 1e-06
HEAD = 128
MIB = 2**20
f32 = jnp.float32
bf16 = jnp.bfloat16
VM = pl.BlockSpec(memory_space=pltpu.VMEM)
SM = pl.BlockSpec(memory_space=pltpu.SMEM)
GELU_A = math.sqrt(2.0 / math.pi)
GELU_B = GELU_A * 0.044715
SCORE_SCALE = 1.0 / math.sqrt(HEAD)
LOG2E = math.log2(math.e)


def nn(a, b):
    return lax.dot_general(a, b, (((1,), (0,)), ((), ())), preferred_element_type=f32)


def nt(a, b):
    return lax.dot_general(a, b, (((1,), (1,)), ((), ())), preferred_element_type=f32)


def tn(a, b):
    return lax.dot_general(a, b, (((0,), (0,)), ((), ())), preferred_element_type=f32)


def shape(dims, dtype):
    return jax.ShapeDtypeStruct(dims, dtype)


def call(kernel, outs, args, flops, exps=0, scratch=(), vmem=48, name=None, in_specs=None, **kw):
    moved = sum(math.prod(a.shape) * a.dtype.itemsize for a in (*args, *outs))
    return pl.pallas_call(
        kernel,
        out_shape=outs,
        in_specs=in_specs or [VM] * len(args),
        out_specs=kw.pop("out_specs", [VM] * len(outs)),
        scratch_shapes=list(scratch),
        compiler_params=pltpu.CompilerParams(vmem_limit_bytes=vmem * MIB),
        cost_estimate=pl.CostEstimate(flops=flops, bytes_accessed=moved, transcendentals=exps),
        name=name,
        **kw,
    )(*args)


def chip_at(sizes, me_ref, rx, rb, ra, sign):
    nx, na, nb = sizes
    x = lax.rem(me_ref[0] + (sign * rx) % nx, nx)
    a = lax.rem(me_ref[1] + (sign * ra) % na, na)
    b = lax.rem(me_ref[2] + (sign * rb) % nb, nb)
    return x, a * nb + b


def blocks_of(sizes):
    nx, na, nb = sizes
    return [(rx, rb, ra) for rx in range(nx) for rb in range(nb) for ra in range(na)]


def row_of(sizes, me_ref, rx, rb, ra, sign, core, shard):
    x, f = chip_at(sizes, me_ref, rx, rb, ra, sign)
    return pl.ds(pl.multiple_of(((x * 2 + core) * (sizes[1] * sizes[2]) + f) * shard, shard), shard)


def assemble(sizes, me_ref, refs, whole_ref):
    nx, na, nb = sizes
    shard = refs[0].shape[0] // na
    for other in range(2):
        core = me_ref[3] if other == 0 else 1 - me_ref[3]
        for rx, rb, ra in blocks_of(sizes):
            ref = refs[(other * nx + rx) * nb + rb]
            whole_ref[row_of(sizes, me_ref, rx, rb, ra, -1, core, shard), :] = ref[ra * shard : (ra + 1) * shard, :]


def hand_out(sizes, me_ref, whole_ref, keep_ref, send_ref, x_outer):
    nx, na, nb = sizes
    shard = keep_ref.shape[0] // (nx * na * nb)
    for other, ref in enumerate((keep_ref, send_ref)):
        core = me_ref[3] if other == 0 else 1 - me_ref[3]
        for rx, rb, ra in blocks_of(sizes):
            at = (((rx * nb + rb) if x_outer else (rb * nx + rx)) * na + ra) * shard
            ref[at : at + shard, :] = whole_ref[row_of(sizes, me_ref, rx, rb, ra, 1, core, shard), :]


def mask_bias(len_ref, first, rows, cols):
    q_pos = first + lax.broadcasted_iota(jnp.int32, (rows, 1), 0)
    k_pos = lax.broadcasted_iota(jnp.int32, (1, cols), 1)
    q_seg = jnp.zeros((rows, 1), jnp.int32)
    k_seg = jnp.zeros((1, cols), jnp.int32)
    end = jnp.int32(0)
    for slot in range(len_ref.shape[1]):
        end = end + len_ref[0, slot]
        q_seg = q_seg + (q_pos >= end).astype(jnp.int32)
        k_seg = k_seg + (k_pos >= end).astype(jnp.int32)
    k_seg = jnp.where(k_pos >= end, -1, k_seg)
    allowed = ((q_seg == k_seg) & (k_pos <= q_pos)) | (k_pos == q_pos)
    return jnp.where(allowed, 0.0, -1e30).astype(f32)


def gain_rows(block):
    return block.astype(f32).T


def norm_tile(x, gain):
    r = lax.rsqrt(jnp.mean(x * x, axis=-1, keepdims=True) + EPS)
    return x * r * gain


def attention_forward_kernel(sizes, me_ref, len_ref, x_ref, *refs):
    *pieces, w_ref, qkv_ref, att_ref, gains, normed, bias = refs
    assemble(sizes, me_ref, pieces, w_ref)
    rows, model = x_ref.shape
    wide = qkv_ref.shape[1]
    heads = (wide - 2 * HEAD) // HEAD
    gains[...] = gain_rows(w_ref[:, wide : wide + HEAD])[:8]

    @pl.loop(0, rows // 128)
    def _(t):
        at = pl.ds(pl.multiple_of(t * 128, 128), 128)
        normed[at, :] = norm_tile(x_ref[at, :].astype(f32), gains[0:1, :]).astype(bf16)

    @pl.loop(0, wide // 256)
    def _(j):
        at = pl.ds(pl.multiple_of(j * 256, 256), 256)
        qkv_ref[:, at] = nn(normed[...], w_ref[:, at]).astype(bf16)

    key_at = heads * HEAD
    for i in range(rows // 128):
        ext = (i + 1) * 128
        q_at = slice(i * 128, ext)
        bias[:, :ext] = mask_bias(len_ref, i * 128, 128, ext)

        @pl.loop(0, heads // 2)
        def _(pair):
            at = pl.ds(pl.multiple_of(pair * 256, 256), 256)
            both = qkv_ref[q_at, at]
            q = jnp.concatenate([both[:, :HEAD], both[:, HEAD:]], axis=0)
            s = nt(q, qkv_ref[:ext, key_at : key_at + HEAD]) * (SCORE_SCALE * LOG2E)
            s = s.reshape(2, 128, ext) + bias[:, :ext][None]
            s = s.reshape(256, ext)
            e = jnp.exp2(s - jnp.max(s, axis=-1, keepdims=True))
            p = e * (1.0 / jnp.sum(e, axis=-1, keepdims=True))
            o = nn(p.astype(bf16), qkv_ref[:ext, key_at + HEAD :]).astype(bf16)
            att_ref[q_at, at] = jnp.concatenate([o[:128], o[128:]], axis=1)


def attention_forward(sizes, me, lengths, x, pieces):
    rows, model = x.shape
    columns = pieces[0].shape[1]
    wide = columns - HEAD
    return call(
        functools.partial(attention_forward_kernel, sizes),
        [shape((model, columns), bf16), shape((rows, wide), bf16), shape((rows, wide - 2 * HEAD), bf16)],
        (me, lengths, x, *pieces),
        2 * rows * model * wide + 4 * rows * rows * model,
        rows * rows * 4,
        [pltpu.VMEM((8, model), f32), pltpu.VMEM((rows, model), bf16), pltpu.VMEM((128, rows), f32)],
        40,
        "attention_forward",
        [SM, SM] + [VM] * (1 + len(pieces)),
    )


def branch_kernel(sizes, me_ref, x_ref, att_ref, w_ref, *refs):
    *pieces, wo_ref, hidden_ref, nt_ref, gains = refs
    assemble(sizes, me_ref, pieces, wo_ref)
    rows = x_ref.shape[0]
    gains[...] = gain_rows(w_ref[...])[:8]
    model = wo_ref.shape[1]

    @pl.loop(0, model // 256)
    def _(j):
        at = pl.ds(pl.multiple_of(j * 256, 256), 256)
        hidden_ref[:, at] = x_ref[:, at].astype(f32) + nn(att_ref[...], wo_ref[:, at])

    @pl.loop(0, rows // 128)
    def _(t):
        at = pl.ds(pl.multiple_of(t * 128, 128), 128)
        nt_ref[at, :] = norm_tile(hidden_ref[at, :], gains[1:2, :]).astype(bf16)


def branch(sizes, me, x, att, w, pieces):
    rows, model = x.shape
    last = w.shape[1] // HEAD - 1
    whole = lambda a: pl.BlockSpec(a.shape, lambda i: (0, 0))
    wo = shape((model, model), bf16)
    return call(
        functools.partial(branch_kernel, sizes),
        [wo, shape((rows, model), f32), shape((rows, model), bf16)],
        (me, x, att, w, *pieces),
        2 * rows * model * model,
        0,
        [pltpu.VMEM((8, model), f32)],
        40,
        "branch",
        [SM, whole(x), whole(att), pl.BlockSpec((model, HEAD), lambda i: (0, last)), *map(whole, pieces)],
        grid=(1,),
        out_specs=[whole(wo), whole(x), whole(x)],
    )


def gelu_both(v):
    v2 = v * v
    t = jnp.tanh(v * (GELU_A + GELU_B * v2))
    h = 0.5 + 0.5 * t
    a = v * h
    return a, h + (a - a * h) * ((2 * GELU_A) + (6 * GELU_B) * v2)


def ffn_kernel(sizes, x_outer, me_ref, nt_o, nt_p, dy_o, dy_p, *refs):
    nx, na, nb = sizes
    pieces, refs = refs[: nx * nb], refs[nx * nb :]
    act_o, act_p, gi_o, gi_p, up_ref, down_ref = refs[:6]
    outs, (gu, gd) = refs[6:-2], refs[-2:]
    part, model = down_ref.shape
    shard = part // (nx * na * nb)
    step = pl.program_id(0)
    tile = act_o.shape[1]

    @pl.when(step == 0)
    def _():
        for rx, rb, ra in blocks_of(sizes):
            ref = pieces[rx * nb + rb]
            at = slice(ra * shard, (ra + 1) * shard)
            for core in range(2):
                up_ref[row_of(sizes, me_ref, rx, rb, ra, -1, core, shard), :] = ref[at, core * part : (core + 1) * part]
            x, f = chip_at(sizes, me_ref, rx, rb, ra, -1)
            down_ref[pl.ds(pl.multiple_of((x * na * nb + f) * shard, shard), shard), :] = ref[at, 2 * part :]

    cols = pl.ds(pl.multiple_of(step * tile, tile), tile)
    for n_ref, y_ref, a_ref, i_ref in ((nt_o, dy_o, act_o, gi_o), (nt_p, dy_p, act_p, gi_p)):
        inner = nn(n_ref[...], up_ref[:, cols])
        ga = nt(y_ref[...], down_ref[cols, :])
        a, slope = gelu_both(inner)
        a_ref[...] = a.astype(bf16)
        i_ref[...] = (ga * slope).astype(bf16)
    gu[:, cols] = (tn(nt_o[...], gi_o[...]) + tn(nt_p[...], gi_p[...])).astype(bf16)
    gd[cols, :] = (tn(act_o[...], dy_o[...]) + tn(act_p[...], dy_p[...])).astype(bf16)

    @pl.when(step == pl.num_programs(0) - 1)
    def _():
        for rx, rb, ra in blocks_of(sizes):
            first, second, count = (rx, rb, nb) if x_outer else (rb, rx, nx)
            at = slice((second * na + ra) * shard, (second * na + ra + 1) * shard)
            for core in range(2):
                outs[first][at, core * part : (core + 1) * part] = gu[row_of(sizes, me_ref, rx, rb, ra, 1, core, shard), :]
            x, f = chip_at(sizes, me_ref, rx, rb, ra, 1)
            outs[first][at, 2 * part :] = gd[pl.ds(pl.multiple_of((x * na * nb + f) * shard, shard), shard), :]


def ffn(sizes, x_outer, me, nt_o, nt_p, dy_o, dy_p, pieces):
    nx, na, nb = sizes
    rows, model = nt_o.shape
    part = model // 2
    tile = 256
    once = pl.BlockSpec((rows, model), lambda c: (0, 0), pipeline_mode=pl.Buffered(1))
    whole = lambda a: pl.BlockSpec(a.shape, lambda c: (0, 0), pipeline_mode=pl.Buffered(1))
    seen = pl.BlockSpec((rows, tile), lambda c: (0, c))
    firsts, lines = (nx, nb) if x_outer else (nb, nx)
    up, down = shape((model, part), bf16), shape((part, model), bf16)
    grads = [shape((part // firsts, 2 * model), bf16)] * firsts
    outs = call(
        functools.partial(ffn_kernel, sizes, x_outer),
        [shape((rows, part), bf16)] * 4 + [up, down] + grads,
        (me, nt_o, nt_p, dy_o, dy_p, *pieces),
        16 * rows * model * part,
        2 * rows * part,
        [pltpu.VMEM((model, part), bf16), pltpu.VMEM((part, model), bf16)],
        44,
        "ffn",
        [SM] + [once] * 4 + [whole(p) for p in pieces],
        grid=(part // tile,),
        out_specs=[seen] * 4 + [whole(up), whole(down), *map(whole, grads)],
    )
    return outs[:4], outs[4], outs[5], outs[6:]


def ffn_sum_kernel(count, *refs):
    acts, gis = refs[:count], refs[count : 2 * count]
    ups, downs = refs[2 * count : 3 * count], refs[3 * count : 4 * count]
    out_ref, gn_ref = refs[4 * count :]
    out = gn = None
    for a, i, d, u in zip(acts, gis, downs, ups):
        o = nn(a[...], d[...])
        n = nt(i[...], u[...])
        out = o if out is None else out + o
        gn = n if gn is None else gn + n
    out_ref[...] = out.astype(bf16)
    gn_ref[...] = gn.astype(bf16)


def ffn_sum(acts, gis, ups, downs):
    rows, part = acts[0].shape
    model = 2 * part
    count = len(acts)
    wide = 256
    held = pl.BlockSpec((rows, part), lambda g: (0, 0), pipeline_mode=pl.Buffered(1))
    out = pl.BlockSpec((rows, wide), lambda g: (0, g))
    return call(
        functools.partial(ffn_sum_kernel, count),
        [shape((rows, model), bf16)] * 2,
        (*acts, *gis, *ups, *downs),
        count * 4 * rows * part * model,
        0,
        (),
        44,
        "ffn_sum",
        [held] * (2 * count)
        + [pl.BlockSpec((wide, part), lambda g: (g, 0))] * count
        + [pl.BlockSpec((part, wide), lambda g: (0, g))] * count,
        grid=(model // wide,),
        out_specs=[out, out],
    )


def branch_backward_kernel(
    sizes, x_outer, me_ref, hidden_ref, gn_o, gn_p, out_o, out_p, dy_ref, wo_ref, w_ref, att_ref,
    output_ref, gh_ref, gatt_ref, gg_ref, keep_ref, send_ref, gains, gb, gwo_ref,
):
    rows, model = hidden_ref.shape
    gains[...] = gain_rows(w_ref[...])[:8]
    gg_ref[...] = jnp.zeros_like(gg_ref)

    @pl.loop(0, rows // 64)
    def _(t):
        at = pl.ds(pl.multiple_of(t * 64, 64), 64)
        h = hidden_ref[at, :]
        output_ref[at, :] = (h + (out_o[at, :].astype(f32) + out_p[at, :].astype(f32))).astype(bf16)
        gn = gn_o[at, :].astype(f32) + gn_p[at, :].astype(f32)
        r = lax.rsqrt(jnp.mean(h * h, axis=-1, keepdims=True) + EPS)
        z = h * r
        gg_ref[1:2, :] += jnp.sum(gn * z, axis=0, keepdims=True)
        g = gn * gains[1:2, :]
        gh = dy_ref[at, :].astype(f32) + r * (g - z * jnp.mean(g * z, axis=-1, keepdims=True))
        gh_ref[at, :] = gh
        gb[at, :] = gh.astype(bf16)

    @pl.loop(0, model // 256)
    def _(j):
        at = pl.ds(pl.multiple_of(j * 256, 256), 256)
        gatt_ref[:, at] = nt(gb[...], wo_ref[at, :]).astype(bf16)
        gwo_ref[:, at] = tn(att_ref[...], gb[:, at]).astype(bf16)

    hand_out(sizes, me_ref, gwo_ref, keep_ref, send_ref, x_outer)


def branch_backward(sizes, x_outer, me, hidden, gn_o, gn_p, out_o, out_p, dy, wo, w, att):
    rows, model = hidden.shape
    last = w.shape[1] // HEAD - 1
    whole = lambda a: pl.BlockSpec(a.shape, lambda i: (0, 0))
    args = (me, hidden, gn_o, gn_p, out_o, out_p, dy, wo, w, att)
    half = shape((model // 2, model), bf16)
    outs = [
        shape((rows, model), bf16),
        shape((rows, model), f32),
        shape((rows, model), bf16),
        shape((8, model), f32),
        half,
        half,
    ]
    return call(
        functools.partial(branch_backward_kernel, sizes, x_outer),
        outs,
        args,
        4 * rows * model * model,
        0,
        [pltpu.VMEM((8, model), f32), pltpu.VMEM((rows, model), bf16), pltpu.VMEM(wo.shape, bf16)],
        56,
        "branch_backward",
        [SM, *map(whole, args[1:8]), pl.BlockSpec((model, HEAD), lambda i: (0, last)), whole(att)],
        grid=(1,),
        out_specs=[*map(whole, outs)],
    )


def attention_backward_kernel(len_ref, qkv_ref, ga_ref, g_ref, bias, dk, dv):
    rows, wide = qkv_ref.shape
    heads = (wide - 2 * HEAD) // HEAD
    key_at = heads * HEAD
    dk[...] = jnp.zeros_like(dk)
    dv[...] = jnp.zeros_like(dv)
    for i in range(rows // 128):
        ext = (i + 1) * 128
        q_at = slice(i * 128, ext)
        bias[:, :ext] = mask_bias(len_ref, i * 128, 128, ext)

        @pl.loop(0, heads // 2)
        def _(pair):
            at = pl.ds(pl.multiple_of(pair * 256, 256), 256)
            both = qkv_ref[q_at, at]
            q = jnp.concatenate([both[:, :HEAD], both[:, HEAD:]], axis=0)
            both = ga_ref[q_at, at]
            ga = jnp.concatenate([both[:, :HEAD], both[:, HEAD:]], axis=0)
            keys = qkv_ref[:ext, key_at : key_at + HEAD]
            s = nt(q, keys) * (SCORE_SCALE * LOG2E)
            s = s.reshape(2, 128, ext) + bias[:, :ext][None]
            s = s.reshape(256, ext)
            e = jnp.exp2(s - jnp.max(s, axis=-1, keepdims=True))
            p = e * (1.0 / jnp.sum(e, axis=-1, keepdims=True))
            gp = nt(ga, qkv_ref[:ext, key_at + HEAD :])
            pg = p * gp
            gs = (pg - p * jnp.sum(pg, axis=-1, keepdims=True)).astype(bf16)
            dv[:ext, :] += tn(p.astype(bf16), ga)
            dk[:ext, :] += tn(gs, q)
            gq = (nn(gs, keys) * SCORE_SCALE).astype(bf16)
            g_ref[q_at, at] = jnp.concatenate([gq[:128], gq[128:]], axis=1)

    g_ref[:, key_at : key_at + HEAD] = (dk[...] * SCORE_SCALE).astype(bf16)
    g_ref[:, key_at + HEAD :] = dv[...].astype(bf16)


def attention_backward(lengths, qkv, ga):
    rows, wide = qkv.shape
    model = ga.shape[1]
    return call(
        attention_backward_kernel,
        [shape(qkv.shape, bf16)],
        (lengths, qkv, ga),
        10 * rows * rows * model,
        rows * rows * 4,
        [pltpu.VMEM((128, rows), f32), pltpu.VMEM((rows, HEAD), f32), pltpu.VMEM((rows, HEAD), f32)],
        40,
        "attention_backward",
        [SM, VM, VM],
    )[0]


def input_backward_kernel(
    sizes, x_outer, me_ref, x_ref, g_ref, w_ref, gh_ref, gg_ref, gx_ref, keep_ref, send_ref, gains, normed, gn, sums, gw_ref
):
    rows, model = x_ref.shape
    wide = g_ref.shape[1]
    gains[...] = gain_rows(w_ref[:, wide : wide + HEAD])[:8]
    sums[...] = jnp.zeros_like(sums)
    sums[0:8, :] = gg_ref[...]

    @pl.loop(0, rows // 128)
    def _(t):
        at = pl.ds(pl.multiple_of(t * 128, 128), 128)
        normed[at, :] = norm_tile(x_ref[at, :].astype(f32), gains[0:1, :]).astype(bf16)

    @pl.loop(0, model // 256)
    def _(j):
        at = pl.ds(pl.multiple_of(j * 256, 256), 256)
        gn[:, at] = nt(g_ref[...], w_ref[at, :wide])

    @pl.loop(0, wide // 256)
    def _(j):
        at = pl.ds(pl.multiple_of(j * 256, 256), 256)
        gw_ref[:, at] = tn(normed[...], g_ref[:, at]).astype(bf16)

    @pl.loop(0, rows // 64)
    def _(t):
        at = pl.ds(pl.multiple_of(t * 64, 64), 64)
        x = x_ref[at, :].astype(f32)
        n = gn[at, :]
        r = lax.rsqrt(jnp.mean(x * x, axis=-1, keepdims=True) + EPS)
        z = x * r
        sums[0:1, :] += jnp.sum(n * z, axis=0, keepdims=True)
        g = n * gains[0:1, :]
        gx_ref[at, :] = (gh_ref[at, :] + r * (g - z * jnp.mean(g * z, axis=-1, keepdims=True))).astype(bf16)

    gw_ref[:, wide : wide + HEAD] = sums[...].T.astype(bf16)
    hand_out(sizes, me_ref, gw_ref, keep_ref, send_ref, x_outer)


def input_backward(sizes, x_outer, me, x, g, w, gh, gg):
    rows, model = x.shape
    wide = g.shape[1]
    half = shape((w.shape[0] // 2, w.shape[1]), bf16)
    return call(
        functools.partial(input_backward_kernel, sizes, x_outer),
        [shape(x.shape, bf16), half, half],
        (me, x, g, w, gh, gg),
        4 * rows * model * wide,
        0,
        [
            pltpu.VMEM((8, model), f32),
            pltpu.VMEM((rows, model), bf16),
            pltpu.VMEM((rows, model), f32),
            pltpu.VMEM((HEAD, model), f32),
            pltpu.VMEM(w.shape, bf16),
        ],
        56,
        "input_backward",
        [SM] + [VM] * 5,
    )


def spread(a, axis, n):
    return [a] + [lax.ppermute(a, axis, [(i, (i + s) % n) for i in range(n)]) for s in range(1, n)]


def add(parts):
    total = parts[0].astype(f32)
    for p in parts[1:]:
        total = total + p.astype(f32)
    return total


def gather_chips(sizes, a, x_first):
    nx, _, nb = sizes
    if x_first:
        by_x = [spread(p, "f2", nb) for p in spread(a, "x", nx)]
        return [by_x[rx][rb] for rx in range(nx) for rb in range(nb)]
    by_b = [spread(p, "x", nx) for p in spread(a, "f2", nb)]
    return [by_b[rb][rx] for rx in range(nx) for rb in range(nb)]


def send_on(parts, axis, n):
    return [lax.ppermute(parts[s], axis, [(i, (i + s) % n) for i in range(n)]) for s in range(1, n)]


def reduce_chips(sizes, parts, x_outer):
    nx, na, nb = sizes
    (first, n1), (second, n2) = (("x", nx), ("f2", nb)) if x_outer else (("f2", nb), ("x", nx))
    got = [parts[0], *send_on(parts, first, n1)]
    cut = lambda a, s, n: a[s * (a.shape[0] // n) : (s + 1) * (a.shape[0] // n)]
    parts = [add([cut(p, s, n2) for p in got]).astype(bf16) for s in range(n2)]
    got = [parts[0], *send_on(parts, second, n2)]
    parts = [add([cut(p, s, na) for p in got]).astype(bf16) for s in range(na)]
    return add([parts[0], *send_on(parts, "f1", na)])


def on_device(
    sizes, tokens, doc_lengths, gain_one, query_weight, key_weight, value_weight, out_weight,
    gain_two, up_weight, down_weight, cotangent,
):
    nx, na, nb = sizes
    fsdp = na * nb
    core = lax.axis_index("core")
    me = jnp.stack([lax.axis_index(a) for a in ("x", "f1", "f2", "core")]).astype(jnp.int32)
    swap = lambda a: lax.ppermute(a, "core", [(0, 1), (1, 0)])
    rows, model = tokens.shape
    shard = query_weight.shape[0]
    ff = up_weight.shape[1]
    chunks = down_weight.shape[0] // shard
    part = ff // (2 * chunks)

    gain_block = jnp.zeros((shard, HEAD), bf16).at[:, 0].set(gain_one).at[:, 1].set(gain_two)
    w_rows = jnp.concatenate([query_weight, key_weight, value_weight, gain_block, out_weight], axis=1)
    columns = w_rows.shape[1] - out_weight.shape[1]
    along = spread(w_rows, "f1", na)
    w_block = jnp.concatenate([a[:, :columns] for a in along], axis=0)
    wo_block = jnp.concatenate([a[:, columns:] for a in along], axis=0)
    w_pieces = gather_chips(sizes, w_block, True)
    wo_pieces = gather_chips(sizes, wo_block, False)
    w_pieces += [swap(p) for p in w_pieces]
    wo_pieces += [swap(p) for p in wo_pieces]

    dy_p = swap(cotangent)
    up = up_weight.reshape(shard, nx, 2, fsdp, chunks, shard).transpose(2, 0, 4, 1, 3, 5)
    up = up.reshape(2, shard, chunks, part)
    up_keep = jnp.where(core == 0, up[0], up[1])
    up_come = swap(jnp.where(core == 0, up[1], up[0]))
    up_pair = jnp.where(core == 0, jnp.stack([up_keep, up_come], 2), jnp.stack([up_come, up_keep], 2))
    up_pair = up_pair.reshape(shard, chunks, 2 * part)
    down = down_weight.reshape(chunks, shard, model)
    f_rows = jnp.concatenate([p for c in range(chunks) for p in (up_pair[:, c], down[c])], axis=1)
    along = spread(f_rows, "f1", na)
    wide = 2 * model
    pieces = []
    for c in range(chunks):
        block = jnp.concatenate([a[:, c * wide : (c + 1) * wide] for a in along], axis=0)
        pieces.append(gather_chips(sizes, block, c % 2 == 0))

    w, qkv, att = attention_forward(sizes, me, doc_lengths, tokens, w_pieces)
    wo, hidden, nt_o = branch(sizes, me, tokens, att, w, wo_pieces)
    nt_p = swap(nt_o)

    acts_o, acts_p, gis_o, gis_p, ups, downs, sums = [], [], [], [], [], [], []
    for c in range(chunks):
        seen, up_c, down_c, grads = ffn(sizes, c % 2 == 0, me, nt_o, nt_p, cotangent, dy_p, pieces[c])
        for kept, a in zip((acts_o, acts_p, gis_o, gis_p), seen):
            kept.append(a)
        ups.append(up_c)
        downs.append(down_c)
        sums.append(reduce_chips(sizes, grads, c % 2 == 0))
    out_p, gn_p = ffn_sum(acts_p, gis_p, ups, downs)
    out_r, gn_r = swap(out_p), swap(gn_p)
    out_o, gn_o = ffn_sum(acts_o, gis_o, ups, downs)

    output, gh, gatt, gg, keep, send = branch_backward(
        sizes, False, me, hidden, gn_o, gn_r, out_o, out_r, cotangent, wo, w, att
    )

    def reduce_all(keep, send, x_outer):
        come = swap(send)
        n = nx if x_outer else nb
        cut = keep.shape[0] // n
        parts = [add([a[s * cut : (s + 1) * cut] for a in (keep, come)]).astype(bf16) for s in range(n)]
        return reduce_chips(sizes, parts, x_outer)

    grad_out = reduce_all(keep, send, False)
    gqkv = attention_backward(doc_lengths, qkv, gatt)
    grad_tokens, keep, send = input_backward(sizes, True, me, tokens, gqkv, w, gh, gg)
    gw = reduce_all(keep, send, True)

    sums = jnp.stack(sums, axis=1)
    grad_down = sums[:, :, model:].transpose(1, 0, 2).reshape(chunks * shard, model)
    g_up = sums[:, :, :model].reshape(shard, chunks, 2, part).astype(bf16)
    keep = jnp.where(core == 0, g_up[:, :, 0], g_up[:, :, 1])
    come = swap(jnp.where(core == 0, g_up[:, :, 1], g_up[:, :, 0]))
    grad_up = jnp.where(core == 0, jnp.stack([keep, come], 0), jnp.stack([come, keep], 0))
    grad_up = grad_up.reshape(2, shard, chunks, nx, fsdp, shard).transpose(1, 3, 0, 4, 2, 5)
    grad_up = grad_up.reshape(shard, ff).astype(f32)

    qw = query_weight.shape[1]
    return (
        output,
        grad_tokens,
        gw[:, qw + 2 * HEAD],
        gw[:, :qw],
        gw[:, qw : qw + HEAD],
        gw[:, qw + HEAD : qw + 2 * HEAD],
        grad_out,
        gw[:, qw + 2 * HEAD + 1],
        grad_up,
        grad_down,
    )


def solution(mesh):
    dp, fsdp = mesh.shape["dp"], mesh.shape["fsdp"]
    sizes = (dp // 2, 4, fsdp // 4)
    names = ("x", "core", "f1", "f2")
    split = Mesh(mesh.devices.reshape(sizes[0], 2, *sizes[1:]), names)
    rows, line = P(names, None), P(names)
    return jax.shard_map(
        functools.partial(on_device, sizes),
        mesh=split,
        in_specs=(rows, rows, line, rows, rows, rows, rows, line, rows, rows, rows),
        out_specs=(rows, rows, line, rows, rows, rows, rows, line, rows, rows),
        check_vma=False,
    )
```

```python
import functools
import math

import jax
import jax.numpy as jnp
from jax import lax
from jax.experimental import pallas as pl
from jax.experimental.pallas import tpu as pltpu
from jax.sharding import Mesh, PartitionSpec as P

EPS = 1e-06
HEAD = 128
MIB = 2**20
f32 = jnp.float32
bf16 = jnp.bfloat16
VM = pl.BlockSpec(memory_space=pltpu.VMEM)
SM = pl.BlockSpec(memory_space=pltpu.SMEM)
GELU_A = math.sqrt(2.0 / math.pi)
GELU_B = GELU_A * 0.044715
SCORE_SCALE = 1.0 / math.sqrt(HEAD)
LOG2E = math.log2(math.e)
MARKS = 64
GROUP = 2
VMEM_MIB = 60
HINT = 8


def nn(a, b):
    return lax.dot_general(a, b, (((1,), (0,)), ((), ())), preferred_element_type=f32)


def nt(a, b):
    return lax.dot_general(a, b, (((1,), (1,)), ((), ())), preferred_element_type=f32)


def tn(a, b):
    return lax.dot_general(a, b, (((0,), (0,)), ((), ())), preferred_element_type=f32)


def shape(dims, dtype):
    return jax.ShapeDtypeStruct(dims, dtype)


def call(kernel, outs, args, flops, exps=0, scratch=(), vmem=48, name=None, in_specs=None, **kw):
    moved = sum(math.prod(a.shape) * a.dtype.itemsize for a in (*args, *outs))
    return pl.pallas_call(
        kernel,
        out_shape=outs,
        in_specs=in_specs or [VM] * len(args),
        out_specs=kw.pop("out_specs", [VM] * len(outs)),
        scratch_shapes=list(scratch),
        compiler_params=pltpu.CompilerParams(vmem_limit_bytes=vmem * MIB),
        cost_estimate=pl.CostEstimate(flops=flops // HINT, bytes_accessed=moved // HINT, transcendentals=exps // HINT),
        name=name,
        **kw,
    )(*args)


def chip_at(sizes, order, me_ref, rx, rb, ra, sign):
    nx, na, nb = sizes
    x = lax.rem(me_ref[0] + (sign * rx) % nx, nx)
    a = lax.rem(me_ref[1] + (sign * ra) % na, na) if order[1] else ra
    b = lax.rem(me_ref[2] + (sign * rb) % nb, nb)
    return x, a * nb + b


def blocks_of(sizes, order):
    nx, na, nb = sizes
    for rx in range(nx):
        for rb in range(nb):
            for ra in range(na):
                yield (rx, rb, ra), (rx, rb) if order[0] else (rb, rx)


def seconds(sizes, order):
    return sizes[2] if order[0] else sizes[0]


def firsts(sizes, order):
    return sizes[0] if order[0] else sizes[2]


def row_of(sizes, x, f, core, shard):
    return pl.ds(pl.multiple_of(((x * 2 + core) * (sizes[1] * sizes[2]) + f) * shard, shard), shard)


def half_row_of(sizes, x, f, shard):
    return pl.ds(pl.multiple_of((x * (sizes[1] * sizes[2]) + f) * shard, shard), shard)


def assemble(sizes, me_ref, orders, refs, whole_ref):
    refs, column = list(refs), 0
    for order in orders:
        count = seconds(sizes, order)
        mine, refs = refs[: 2 * count], refs[2 * count :]
        width = mine[0].shape[1]
        shard = mine[0].shape[0] // (firsts(sizes, order) * sizes[1])
        for other in range(2):
            core = me_ref[3] if other == 0 else 1 - me_ref[3]
            for place, (first, second) in blocks_of(sizes, order):
                x, f = chip_at(sizes, order, me_ref, *place, -1)
                at = (first * sizes[1] + place[2]) * shard
                whole_ref[row_of(sizes, x, f, core, shard), column : column + width] = mine[other * count + second][at : at + shard, :]
        column += width


def hand_out(sizes, me_ref, orders, whole_ref, refs):
    nx, na, nb = sizes
    column = 0
    for n, order in enumerate(orders):
        for other, ref in enumerate(refs[2 * n : 2 * n + 2]):
            core = me_ref[3] if other == 0 else 1 - me_ref[3]
            shard = ref.shape[0] // (nx * na * nb)
            for place, (first, second) in blocks_of(sizes, order):
                x, f = chip_at(sizes, order, me_ref, *place, 1)
                at = ((first * seconds(sizes, order) + second) * na + place[2]) * shard
                ref[at : at + shard, :] = whole_ref[row_of(sizes, x, f, core, shard), column : column + ref.shape[1]]
        column += refs[2 * n].shape[1]


def gain_rows(block):
    return block.astype(f32).T


def norm_tile(x, gain):
    r = lax.rsqrt(jnp.mean(x * x, axis=-1, keepdims=True) + EPS)
    return x * r * gain


def position_ids(len_ref, pos):
    seg = jnp.zeros(pos.shape, jnp.int32)
    end = jnp.int32(0)
    slots = len_ref.shape[1]
    for slot in range(slots):
        end = end + len_ref[0, slot]
        seg = seg + (pos >= end).astype(jnp.int32)
    return jnp.where(pos >= end, slots + pos // 128, seg), pos >= end


def query_marks(len_ref, first):
    pos = first + lax.broadcasted_iota(jnp.int32, (128, 1), 0)
    ids, _ = position_ids(len_ref, pos)
    lane = lax.broadcasted_iota(jnp.int32, (128, 128), 1)
    return jnp.where(lane == ids, 1.0, 0.0)


def key_marks(len_ref, first):
    pos = first + lax.broadcasted_iota(jnp.int32, (128, 1), 0)
    ids, _ = position_ids(len_ref, pos)
    lane = lax.broadcasted_iota(jnp.int32, (128, 128), 1)
    return jnp.where(lane >= MARKS, 1.0, jnp.where(lane == ids, 0.0, -1e30)).astype(bf16)


def block_bias(len_ref, first):
    q_pos = first + lax.broadcasted_iota(jnp.int32, (128, 1), 0)
    k_pos = first + lax.broadcasted_iota(jnp.int32, (1, 128), 1)
    _, k_pad = position_ids(len_ref, k_pos)
    allowed = ((k_pos <= q_pos) & jnp.logical_not(k_pad)) | (k_pos == q_pos)
    return jnp.where(allowed, 0.0, -1e30)


def split3(v):
    hi = v.astype(bf16).astype(f32)
    mid = (v - hi).astype(bf16).astype(f32)
    return hi, mid, v - hi - mid


def at_lanes(base, first, values):
    lane = lax.broadcasted_iota(jnp.int32, base.shape, 1)
    for n, v in enumerate(values):
        base = jnp.where(lane == first + n, v, base)
    return base


def stack(a, heads):
    return jnp.concatenate([a[:, h * HEAD : (h + 1) * HEAD] for h in range(heads)], axis=0)


def project_kernel(sizes, orders, me_ref, x_ref, *refs):
    *pieces, w_ref, qkv_ref, gains_ref, normed = refs
    assemble(sizes, me_ref, orders, pieces, w_ref)
    rows = x_ref.shape[0]
    wide = qkv_ref.shape[1]
    key_at = wide - 2 * HEAD
    gains_ref[...] = gain_rows(w_ref[:, wide : wide + HEAD])[:8]

    @pl.loop(0, rows // 128, unroll=True)
    def _(t):
        at = pl.ds(pl.multiple_of(t * 128, 128), 128)
        normed[at, :] = norm_tile(x_ref[at, :].astype(f32), gains_ref[0:1, :]).astype(bf16)

    @pl.loop(0, key_at // 256, unroll=True)
    def _(j):
        at = pl.ds(pl.multiple_of(j * 256, 256), 256)
        qkv_ref[:, at] = (nn(normed[...], w_ref[:, at]) * (SCORE_SCALE * LOG2E)).astype(bf16)

    qkv_ref[:, key_at:] = nn(normed[...], w_ref[:, key_at:wide]).astype(bf16)


def project(sizes, orders, columns, me, x, pieces):
    rows, model = x.shape
    wide = columns - HEAD
    return call(
        functools.partial(project_kernel, sizes, orders),
        [shape((model, columns), bf16), shape((rows, wide), bf16), shape((8, model), f32)],
        (me, x, *pieces),
        2 * rows * model * wide,
        0,
        [pltpu.VMEM((rows, model), bf16)],
        VMEM_MIB,
        "project",
        [SM] + [VM] * (1 + len(pieces)),
    )


def marked(len_ref, qkv_ref, keys, values):
    rows, wide = qkv_ref.shape
    keys[:, :HEAD] = qkv_ref[:, wide - 2 * HEAD : wide - HEAD]
    values[:, :HEAD] = qkv_ref[:, wide - HEAD :]

    @pl.loop(0, rows // 128, unroll=True)
    def _(t):
        at = pl.ds(pl.multiple_of(t * 128, 128), 128)
        keys[at, HEAD:] = key_marks(len_ref, t * 128)
        values[at, HEAD:] = jnp.ones((128, HEAD), bf16)


def attention_forward_kernel(len_ref, qkv_ref, att_ref, lse_ref, keys, values):
    rows, wide = qkv_ref.shape
    heads = (wide - 2 * HEAD) // HEAD
    marked(len_ref, qkv_ref, keys, values)

    for i in range(rows // 128):
        ext = (i + 1) * 128
        q_at = slice(i * 128, ext)
        marks = query_marks(len_ref, i * 128).astype(bf16)
        bias = block_bias(len_ref, i * 128)
        lse = jnp.zeros((128, HEAD), f32)
        lane = lax.broadcasted_iota(jnp.int32, (128, HEAD), 1)
        for first in range(0, heads, GROUP):
            cols = slice(first * HEAD, (first + GROUP) * HEAD)
            q = stack(qkv_ref[q_at, cols], GROUP)
            q = jnp.concatenate([q, jnp.concatenate([marks] * GROUP, axis=0)], axis=1)
            s = nt(q, keys[:ext, :])
            last = s[:, ext - 128 :] + jnp.concatenate([bias] * GROUP, axis=0)
            s = jnp.concatenate([s[:, : ext - 128], last], axis=1) if i else last
            peak = jnp.max(s, axis=-1, keepdims=True)
            e = jnp.exp2(s - peak).astype(bf16)
            o = nn(e, values[:ext, :])
            total = o[:, HEAD:]
            low = peak + jnp.log2(total)
            o = (o[:, :HEAD] / total).astype(bf16)
            att_ref[q_at, cols] = jnp.concatenate([o[h * 128 : (h + 1) * 128] for h in range(GROUP)], axis=1)
            for h in range(GROUP):
                lse = jnp.where(lane == first + h, low[h * 128 : (h + 1) * 128], lse)
        lse_ref[q_at, :] = lse


def attention_forward(lengths, qkv):
    rows, wide = qkv.shape
    model = wide - 2 * HEAD
    return call(
        attention_forward_kernel,
        [shape((rows, model), bf16), shape((rows, HEAD), f32)],
        (lengths, qkv),
        4 * rows * rows * model,
        rows * rows * 4,
        [pltpu.VMEM((rows, 2 * HEAD), bf16), pltpu.VMEM((rows, 2 * HEAD), bf16)],
        VMEM_MIB,
        "attention_forward",
        [SM, VM],
    )


def branch_kernel(sizes, orders, me_ref, x_ref, att_ref, gains_ref, *refs):
    *pieces, wo_ref, hidden_ref, nt_ref = refs

    @pl.when(pl.program_id(0) == 0)
    def _():
        assemble(sizes, me_ref, orders, pieces, wo_ref)

    hidden_ref[...] = x_ref[...].astype(f32) + nn(att_ref[...], wo_ref[...])

    @pl.loop(0, x_ref.shape[0] // 128, unroll=True)
    def _(t):
        at = pl.ds(pl.multiple_of(t * 128, 128), 128)
        nt_ref[at, :] = norm_tile(hidden_ref[at, :], gains_ref[1:2, :]).astype(bf16)


def held(a):
    return pl.BlockSpec(a.shape, lambda i: (0, 0), pipeline_mode=pl.Buffered(1))


def branch(sizes, orders, me, x, att, gains, pieces):
    rows, model = x.shape
    tile = rows // 4
    wo = shape((model, model), bf16)
    strip = pl.BlockSpec((tile, model), lambda i: (i, 0))
    return call(
        functools.partial(branch_kernel, sizes, orders),
        [wo, shape((rows, model), f32), shape((rows, model), bf16)],
        (me, x, att, gains, *pieces),
        2 * rows * model * model,
        0,
        (),
        VMEM_MIB,
        "branch",
        [SM, strip, strip, held(gains), *map(held, pieces)],
        grid=(rows // tile,),
        out_specs=[held(wo), strip, strip],
    )


def gelu_both(v):
    v2 = v * v
    t = jnp.tanh(v * (GELU_A + GELU_B * v2))
    h = 0.5 + 0.5 * t
    a = v * h
    return a, h + (a - a * h) * ((2 * GELU_A) + (6 * GELU_B) * v2)


def ffn_kernel(sizes, order, me_ref, *refs):
    count, lines = seconds(sizes, order), firsts(sizes, order)
    take = lambda n: [refs.pop(0) for _ in range(n)]
    refs = list(refs)
    ins = take(4 + count)
    seen, whole, outs = take(4), take(2), take(lines)
    held_in = take(4 + count)
    acts, (up_ref, down_ref), (gu, gd), staged = take(4), take(2), take(2), take(lines)
    in_sem, out_sem = refs
    part, model = down_ref.shape
    shard = part // math.prod(sizes)
    tile = min(256, part)

    loads = [pltpu.make_async_copy(a, b, in_sem.at[n]) for n, (a, b) in enumerate(zip(ins, held_in))]
    for n in (*range(4, 4 + count), 0, 2, 1, 3):
        loads[n].start()
    started = []

    def store(src, dst):
        copy = pltpu.make_async_copy(src, dst, out_sem.at[len(started)])
        copy.start()
        started.append(copy)

    pieces = held_in[4:]
    for n in range(count):
        loads[4 + n].wait()
    for place, (first, second) in blocks_of(sizes, order):
        x, f = chip_at(sizes, order, me_ref, *place, -1)
        row = (first * sizes[1] + place[2]) * shard
        at = slice(row, row + shard)
        for core in range(2):
            up_ref[row_of(sizes, x, f, core, shard), :] = pieces[second][at, core * part : (core + 1) * part]
        down_ref[half_row_of(sizes, x, f, shard), :] = pieces[second][at, 2 * part :]
    store(up_ref, whole[0])
    store(down_ref, whole[1])

    nt_o, nt_p, dy_o, dy_p = held_in[:4]
    act_o, act_p, gi_o, gi_p = acts
    tiles = [slice(j * tile, (j + 1) * tile) for j in range(part // tile)]
    for j, cols in enumerate(tiles):
        for own, (n_ref, y_ref, a_ref, i_ref) in enumerate(((nt_o, dy_o, act_o, gi_o), (nt_p, dy_p, act_p, gi_p))):
            if j == 0:
                loads[own].wait()
            inner = nn(n_ref[...], up_ref[:, cols])
            if j == 0:
                loads[2 + own].wait()
            ga = nt(y_ref[...], down_ref[cols, :])
            a, slope = gelu_both(inner)
            a_ref[:, cols] = a.astype(bf16)
            i_ref[:, cols] = (ga * slope).astype(bf16)
    for n, a in enumerate(acts):
        store(a, seen[n])
    for cols in tiles:
        gu[:, cols] = (tn(nt_o[...], gi_o[:, cols]) + tn(nt_p[...], gi_p[:, cols])).astype(bf16)
    for cols in tiles:
        gd[cols, :] = (tn(act_o[:, cols], dy_o[...]) + tn(act_p[:, cols], dy_p[...])).astype(bf16)

    for line in reversed(range(lines)):
        for place, (first, second) in blocks_of(sizes, order):
            if first != line:
                continue
            x, f = chip_at(sizes, order, me_ref, *place, 1)
            row = (second * sizes[1] + place[2]) * shard
            at = slice(row, row + shard)
            for core in range(2):
                staged[line][at, core * part : (core + 1) * part] = gu[row_of(sizes, x, f, core, shard), :]
            staged[line][at, 2 * part :] = gd[half_row_of(sizes, x, f, shard), :]
        store(staged[line], outs[line])
    for copy in started:
        copy.wait()


def ffn(sizes, order, me, nt_o, nt_p, dy_o, dy_p, pieces):
    rows, model = nt_o.shape
    part = model // 2
    up, down = shape((model, part), bf16), shape((part, model), bf16)
    lines = firsts(sizes, order)
    grads = [shape((part // lines, 2 * model), bf16)] * lines
    ins = (nt_o, nt_p, dy_o, dy_p, *pieces)
    outs = [shape((rows, part), bf16)] * 4 + [up, down] + grads
    far = pl.BlockSpec(memory_space=pl.ANY)
    outs = call(
        functools.partial(ffn_kernel, sizes, order),
        outs,
        (me, *ins),
        16 * rows * model * part,
        2 * rows * part,
        [pltpu.VMEM(a.shape, bf16) for a in (*ins, *outs[:4], up, down, up, down, *grads)]
        + [pltpu.SemaphoreType.DMA((len(ins),)), pltpu.SemaphoreType.DMA((len(outs),))],
        VMEM_MIB,
        "ffn",
        [SM] + [far] * len(ins),
        out_specs=[far] * len(outs),
    )
    return outs[:4], outs[4], outs[5], outs[6:]


def hidden_backward_kernel(count, *refs):
    gis, ups, gn_ref = refs[:count], refs[count : 2 * count], refs[2 * count]
    total = None
    for i, u in zip(gis, ups):
        v = nt(i[...], u[...])
        total = v if total is None else total + v
    gn_ref[...] = total.astype(bf16)


def hidden_backward(gis, ups):
    rows, part = gis[0].shape
    model = ups[0].shape[0]
    count = len(gis)
    tile = model // 4
    return call(
        functools.partial(hidden_backward_kernel, count),
        [shape((rows, model), bf16)],
        (*gis, *ups),
        count * 2 * rows * part * model,
        0,
        (),
        VMEM_MIB,
        "hidden_backward",
        [pl.BlockSpec((tile, part), lambda g: (g, 0))] * count + [held(u) for u in ups],
        grid=(rows // tile,),
        out_specs=[pl.BlockSpec((tile, model), lambda g: (g, 0))],
    )[0]


def down_kernel(count, *refs):
    acts, downs, more, out_ref = refs[:count], refs[count : 2 * count], refs[2 * count : -1], refs[-1]
    total = None
    for a, d in zip(acts, downs):
        v = nn(a[...], d[...])
        total = v if total is None else total + v
    for m in more:
        total = total + m[...].astype(f32)
    out_ref[...] = total.astype(bf16)


def down(acts, downs, more):
    rows, part = acts[0].shape
    model = downs[0].shape[1]
    count = len(acts)
    tile = rows // 4
    strip = pl.BlockSpec((tile, model), lambda g: (g, 0))
    return call(
        functools.partial(down_kernel, count),
        [shape((rows, model), bf16)],
        (*acts, *downs, *more),
        count * 2 * rows * part * model,
        0,
        (),
        VMEM_MIB,
        "down",
        [pl.BlockSpec((tile, part), lambda g: (g, 0))] * count + [held(d) for d in downs] + [strip] * len(more),
        grid=(rows // tile,),
        out_specs=[strip],
    )[0]


def branch_backward_kernel(sizes, orders, count, me_ref, hidden_ref, gn_ref, dy_ref, att_ref, gains_ref, wo_ref, *refs):
    gis, ups, refs = refs[:count], refs[count : 2 * count], refs[2 * count :]
    gh_ref, gatt_ref, gg_ref, *halves, gn, gb, gwo, low = refs
    step = pl.program_id(0)
    rows = hidden_ref.shape[0]

    @pl.when(step == 0)
    def _():
        gg_ref[...] = jnp.zeros_like(gg_ref)
        gwo[...] = jnp.zeros_like(gwo)

    total = gn_ref[...].astype(f32)
    for i, u in zip(gis, ups):
        total = total + nt(i[...], u[...])
    gn[...] = total

    @pl.loop(0, rows // 64, unroll=True)
    def _(t):
        at = pl.ds(pl.multiple_of(t * 64, 64), 64)
        h, n = hidden_ref[at, :], gn[at, :]
        r = lax.rsqrt(jnp.mean(h * h, axis=-1, keepdims=True) + EPS)
        z = h * r
        gg_ref[1:2, :] += jnp.sum(n * z, axis=0, keepdims=True)
        g = n * gains_ref[1:2, :]
        gh = dy_ref[at, :].astype(f32) + r * (g - z * jnp.mean(g * z, axis=-1, keepdims=True))
        gh_ref[at, :] = gh
        gb[at, :] = gh.astype(bf16)

    gatt_ref[...] = nt(gb[...], wo_ref[...]).astype(bf16)
    gwo[...] += tn(att_ref[...], gb[...])

    @pl.when(step == pl.num_programs(0) - 1)
    def _():
        low[...] = gwo[...].astype(bf16)
        hand_out(sizes, me_ref, orders, low, halves)


def branch_backward(sizes, orders, me, hidden, gn, dy, att, gains, wo, gis, ups):
    rows, model = hidden.shape
    part = gis[0].shape[1]
    count = len(gis)
    tile = rows // 4
    strip = pl.BlockSpec((tile, model), lambda i: (i, 0))
    gg = shape((8, model), f32)
    halves = [shape((model // 2, model // len(orders)), bf16)] * (2 * len(orders))
    return call(
        functools.partial(branch_backward_kernel, sizes, orders, count),
        [shape((rows, model), f32), shape((rows, model), bf16), gg, *halves],
        (me, hidden, gn, dy, att, gains, wo, *gis, *ups),
        4 * rows * model * model + count * 2 * rows * part * model,
        0,
        [
            pltpu.VMEM((tile, model), f32),
            pltpu.VMEM((tile, model), bf16),
            pltpu.VMEM((model, model), f32),
            pltpu.VMEM((model, model), bf16),
        ],
        VMEM_MIB,
        "branch_backward",
        [SM, strip, strip, strip, strip, held(gains), held(wo)]
        + [pl.BlockSpec((tile, part), lambda i: (i, 0))] * count
        + [held(u) for u in ups],
        grid=(rows // tile,),
        out_specs=[strip, strip, held(gg), *map(held, halves)],
    )


def attention_backward_kernel(
    len_ref, qkv_ref, ga_ref, att_ref, lse_ref, g_ref, keys, values, probs, gscores, dk, dv
):
    rows, wide = qkv_ref.shape
    heads = (wide - 2 * HEAD) // HEAD
    key_at = heads * HEAD
    dk[...] = jnp.zeros_like(dk)
    dv[...] = jnp.zeros_like(dv)
    marked(len_ref, qkv_ref, keys, values)

    for i in range(rows // 128):
        ext = (i + 1) * 128
        q_at = slice(i * 128, ext)
        marks = query_marks(len_ref, i * 128)
        bias = block_bias(len_ref, i * 128)
        for first in range(0, heads, GROUP):
            cols = slice(first * HEAD, (first + GROUP) * HEAD)
            q = stack(qkv_ref[q_at, cols], GROUP)
            ga = stack(ga_ref[q_at, cols], GROUP)
            q_more, ga_more = [], []
            for h in range(first, first + GROUP):
                at = slice(h * HEAD, (h + 1) * HEAD)
                q_more.append(at_lanes(marks, MARKS, split3(-lse_ref[q_at, h : h + 1])).astype(bf16))
                delta = jnp.sum(ga_ref[q_at, at].astype(f32) * att_ref[q_at, at].astype(f32), axis=-1, keepdims=True)
                ga_more.append(at_lanes(jnp.zeros((128, HEAD), f32), 0, split3(-delta)).astype(bf16))
            s = nt(jnp.concatenate([q, jnp.concatenate(q_more, axis=0)], axis=1), keys[:ext, :])
            gp = nt(jnp.concatenate([ga, jnp.concatenate(ga_more, axis=0)], axis=1), values[:ext, :])
            last = s[:, ext - 128 :] + jnp.concatenate([bias] * GROUP, axis=0)
            s = jnp.concatenate([s[:, : ext - 128], last], axis=1) if i else last
            p = jnp.exp2(s)
            out = slice(first * 128, (first + GROUP) * 128)
            probs[out, :ext] = p.astype(bf16)
            gscores[out, :ext] = (p * gp).astype(bf16)
        dv[:ext, :] += tn(probs[:, :ext], stack(ga_ref[q_at, :], heads))
        dk[:ext, :] += tn(gscores[:, :ext], stack(qkv_ref[q_at, :key_at], heads))
        gq = (nn(gscores[:, :ext], keys[:ext, :HEAD]) * SCORE_SCALE).astype(bf16)
        g_ref[q_at, :key_at] = jnp.concatenate([gq[h * 128 : (h + 1) * 128] for h in range(heads)], axis=1)

    g_ref[:, key_at : key_at + HEAD] = (dk[...] * (1.0 / LOG2E)).astype(bf16)
    g_ref[:, key_at + HEAD :] = dv[...].astype(bf16)


def attention_backward(lengths, qkv, ga, att, lse):
    rows, wide = qkv.shape
    model = ga.shape[1]
    return call(
        attention_backward_kernel,
        [shape(qkv.shape, bf16)],
        (lengths, qkv, ga, att, lse),
        10 * rows * rows * model,
        rows * rows * 4,
        [
            pltpu.VMEM((rows, 2 * HEAD), bf16),
            pltpu.VMEM((rows, 2 * HEAD), bf16),
            pltpu.VMEM((model, rows), bf16),
            pltpu.VMEM((model, rows), bf16),
            pltpu.VMEM((rows, HEAD), f32),
            pltpu.VMEM((rows, HEAD), f32),
        ],
        VMEM_MIB,
        "attention_backward",
        [SM] + [VM] * 4,
    )[0]


def projection_grads_kernel(sizes, orders, me_ref, x_ref, g_ref, w_ref, gains_ref, gg_ref, *refs):
    *halves, normed, gw = refs
    rows, model = x_ref.shape
    wide = g_ref.shape[1]

    @pl.loop(0, rows // 128, unroll=True)
    def _(t):
        at = pl.ds(pl.multiple_of(t * 128, 128), 128)
        normed[at, :] = norm_tile(x_ref[at, :].astype(f32), gains_ref[0:1, :]).astype(bf16)

    dots = jnp.zeros((model, HEAD), f32)
    for j in range(wide // 256):
        at = slice(j * 256, (j + 1) * 256)
        v = tn(normed[...], g_ref[:, at])
        gw[:, at] = v.astype(bf16)
        v = v * w_ref[:, at].astype(f32)
        dots = dots + (v[:, :HEAD] + v[:, HEAD:])
    one = jnp.sum(dots, axis=-1, keepdims=True) / w_ref[:, wide : wide + 1].astype(f32)
    two = jnp.concatenate([gg_ref[...], jnp.zeros((HEAD - 8, model), f32)], axis=0).T
    lane = lax.broadcasted_iota(jnp.int32, (model, HEAD), 1)
    gw[:, wide : wide + HEAD] = jnp.where(lane == 0, one, two).astype(bf16)
    hand_out(sizes, me_ref, orders, gw, halves)


def projection_grads(sizes, orders, widths, me, x, g, w, gains, gg):
    rows, model = x.shape
    halves = [shape((w.shape[0] // 2, width), bf16) for width in widths for _ in range(2)]
    return call(
        functools.partial(projection_grads_kernel, sizes, orders),
        halves,
        (me, x, g, w, gains, gg),
        2 * rows * model * g.shape[1],
        0,
        [pltpu.VMEM((rows, model), bf16), pltpu.VMEM(w.shape, bf16)],
        VMEM_MIB,
        "projection_grads",
        [SM] + [VM] * 5,
    )


def input_backward_kernel(x_ref, g_ref, gh_ref, w_ref, gains_ref, gx_ref, gn):
    rows = x_ref.shape[0]
    gn[...] = nt(g_ref[...], w_ref[:, : g_ref.shape[1]])

    @pl.loop(0, rows // 64, unroll=True)
    def _(t):
        at = pl.ds(pl.multiple_of(t * 64, 64), 64)
        x = x_ref[at, :].astype(f32)
        r = lax.rsqrt(jnp.mean(x * x, axis=-1, keepdims=True) + EPS)
        z = x * r
        g = gn[at, :] * gains_ref[0:1, :]
        gx_ref[at, :] = (gh_ref[at, :] + r * (g - z * jnp.mean(g * z, axis=-1, keepdims=True))).astype(bf16)


def input_backward(x, g, gh, w, gains):
    rows, model = x.shape
    tile = rows // 4
    strip = lambda a: pl.BlockSpec((tile, a.shape[1]), lambda i: (i, 0))
    return call(
        input_backward_kernel,
        [shape(x.shape, bf16)],
        (x, g, gh, w, gains),
        2 * rows * model * g.shape[1],
        0,
        [pltpu.VMEM((tile, model), f32)],
        VMEM_MIB,
        "input_backward",
        [strip(x), strip(g), strip(gh), held(w), held(gains)],
        grid=(rows // tile,),
        out_specs=[strip(x)],
    )[0]


def after(a, *first):
    return lax.optimization_barrier((a, *first))[0]


def spread(a, axis, n):
    return [a] + [lax.ppermute(a, axis, [(i, (i + s) % n) for i in range(n)]) for s in range(1, n)]


def add(parts):
    total = parts[0].astype(f32)
    for p in parts[1:]:
        total = total + p.astype(f32)
    return total


def send_on(parts, axis, n):
    return [lax.ppermute(parts[s], axis, [(i, (i + s) % n) for i in range(n)]) for s in range(1, n)]


def cut(a, s, n):
    rows = a.shape[0] // n
    return a[s * rows : (s + 1) * rows]


def cut_columns(a, s, n):
    columns = a.shape[1] // n
    return a[:, s * columns : (s + 1) * columns]


class Hops:
    def __init__(self, sizes, order):
        x, b = ("x", sizes[0]), ("f2", sizes[2])
        self.axes = (x, b) if order[0] else (b, x)

    def gather_one(self, block):
        self.lines = spread(block, *self.axes[0])
        return self.lines[1:]

    def gather_two(self):
        self.pieces = spread(jnp.concatenate(self.lines, axis=0), *self.axes[1])
        return self.pieces

    def reduce_one(self, parts):
        self.got = [parts[0], *send_on(parts, *self.axes[0])]

    def reduce_two(self):
        n = self.axes[1][1]
        parts = [add([cut(p, s, n) for p in self.got]).astype(bf16) for s in range(n)]
        self.got = [parts[0], *send_on(parts, *self.axes[1])]
        return parts

    def sum_two(self, n=1):
        return [add([cut(p, s, n) for p in self.got]).astype(bf16) for s in range(n)]


def on_device(
    sizes, tokens, doc_lengths, gain_one, query_weight, key_weight, value_weight, out_weight,
    gain_two, up_weight, down_weight, cotangent,
):
    nx, na, nb = sizes
    fsdp = na * nb
    core = lax.axis_index("core")
    me = jnp.stack([lax.axis_index(a) for a in ("x", "f1", "f2", "core")]).astype(jnp.int32)
    swap = lambda a: lax.ppermute(a, "core", [(0, 1), (1, 0)])
    rows, model = tokens.shape
    shard = query_weight.shape[0]
    ff = up_weight.shape[1]
    chunks = down_weight.shape[0] // shard
    part = ff // (2 * chunks)
    wide = 2 * model
    x_then, b_then = (True, True), (False, True)
    by_index = [(c % 2 == 0, False) for c in range(chunks)]

    lane = lax.broadcasted_iota(jnp.int32, (shard, HEAD), 1)
    gain_block = jnp.where(lane == 0, gain_one[:, None], jnp.where(lane == 1, gain_two[:, None], jnp.zeros((), bf16)))
    w_rows = jnp.concatenate([query_weight, key_weight, value_weight, gain_block], axis=1)
    columns = w_rows.shape[1]
    first_share = columns // 256 * HEAD
    w_orders, w_widths = (x_then, b_then), (first_share, columns - first_share)
    w_along = spread(w_rows, "f1", na)

    up = up_weight.reshape(shard, nx, 2, fsdp, chunks, shard).transpose(2, 0, 4, 1, 3, 5)
    up = up.reshape(2, shard, chunks, part)
    up_keep = jnp.where(core == 0, up[0], up[1])
    up_come = swap(jnp.where(core == 0, up[1], up[0]))
    up_pair = jnp.where(core == 0, jnp.stack([up_keep, up_come], 2), jnp.stack([up_come, up_keep], 2))
    up_pair = up_pair.reshape(shard, chunks, wide // 2)
    down_rows = down_weight.reshape(chunks, shard, model)
    f_along = []
    for first in range(0, chunks, 2):
        mine = jnp.concatenate([p for c in (first, first + 1) for p in (up_pair[:, c], down_rows[c])], axis=1)
        f_along.append(lax.all_gather(after(mine, *w_along[1:]), "f1", axis=0, tiled=True))

    w_block = jnp.concatenate(w_along, axis=0)
    w_hops = [Hops(sizes, order) for order in w_orders]
    lines = w_hops[0].gather_one(w_block[:, :first_share]) + w_hops[1].gather_one(w_block[:, first_share:])
    wo_along = spread(after(out_weight, *lines), "f1", na)
    w_pieces = []
    for h in w_hops:
        p = h.gather_two()
        w_pieces += p + [swap(a) for a in p]
    wo_orders = (x_then, b_then)
    wo_block = jnp.concatenate(wo_along, axis=0)
    wo_hops = [Hops(sizes, order) for order in wo_orders]
    for n, h in enumerate(wo_hops):
        h.gather_one(cut_columns(wo_block, n, 2))
    wo_pieces = []
    for h in wo_hops:
        p = h.gather_two()
        wo_pieces += p + [swap(a) for a in p]
    hops = [Hops(sizes, order) for order in by_index]
    f_lines = lambda c: hops[c].gather_one(cut_columns(f_along[c // 2], c % 2, 2))

    w, qkv, gains = project(sizes, w_orders, columns, me, tokens, w_pieces)
    lines = [p for c in (0, 1) for p in f_lines(c)]
    att, lse = attention_forward(doc_lengths, after(qkv, *lines))
    pieces = {c: hops[c].gather_two() for c in (0, 1)}
    dy_p = swap(after(cotangent, qkv))
    wo, hidden, nt_o = branch(sizes, wo_orders, me, tokens, att, gains, wo_pieces)
    nt_p = swap(nt_o)

    acts_o, acts_p, gis_o, gis_p, ups, downs = [], [], [], [], [], []

    def run_ffn(c, *first):
        seen, up_c, down_c, grads = ffn(sizes, by_index[c], me, after(nt_o, *first), nt_p, cotangent, dy_p, pieces[c])
        for kept, a in zip((acts_o, acts_p, gis_o, gis_p), seen):
            kept.append(a)
        ups.append(up_c)
        downs.append(down_c)
        hops[c].reduce_one(grads)

    def sum_cores(keep, come, order):
        n = firsts(sizes, order)
        return [add([cut(a, s, n) for a in (keep, come)]).astype(bf16) for s in range(n)]

    f_along[1] = after(f_along[1], att)
    lines = [p for c in (2, 3) for p in f_lines(c)]
    run_ffn(0, *pieces[1])
    run_ffn(1, *lines, ups[0])
    for c in (2, 3):
        pieces[c] = hops[c].gather_two()
    run_ffn(2, ups[1])
    ready = hops[0].reduce_two()
    run_ffn(3, *ready, ups[2])
    ready = hops[1].reduce_two()
    gn_p = hidden_backward([after(gis_p[0], *ready), *gis_p[1:]], ups)
    gn_r = swap(gn_p)
    ready = hops[2].reduce_two()
    out_p = down([after(acts_p[0], gn_p, *ready), *acts_p[1:]], downs, [])
    out_r = swap(out_p)
    last = lambda a: lax.psum_scatter(a, "f1", scatter_dimension=0, tiled=True)
    pair = jnp.concatenate([hops[c].sum_two()[0] for c in (0, 1)], axis=1)
    sums = [last(pair)]
    gh, gatt, gg, *halves = branch_backward(
        sizes, wo_orders[:1], me, hidden, gn_r, cotangent, att, gains, wo, [after(gis_o[0], out_p, pair), *gis_o[1:]], ups
    )
    come = swap(halves[1])
    ready = hops[3].reduce_two()
    wo_reduce = Hops(sizes, x_then)
    ready += sum_cores(halves[0], come, x_then)
    wo_reduce.reduce_one(ready[-firsts(sizes, x_then) :])
    g = attention_backward(doc_lengths, after(qkv, *ready), gatt, att, lse)
    ready = wo_reduce.reduce_two()
    pair = jnp.concatenate([hops[c].sum_two()[0] for c in (2, 3)], axis=1)
    sums.append(last(pair))
    halves = projection_grads(sizes, w_orders, w_widths, me, after(tokens, *ready, pair), g, w, gains, gg)
    come = [swap(h) for h in halves[1::2]]
    wo_parts = wo_reduce.sum_two(na)
    wo_got = send_on(wo_parts, "f1", na)
    ready = [sum_cores(k, c, o) for k, c, o in zip(halves[0::2], come, w_orders)]
    w_reduce = [Hops(sizes, order) for order in w_orders]
    for h, r in zip(w_reduce, ready):
        h.reduce_one(r)
    ready = [r for rs in ready for r in rs]
    grad_tokens = input_backward(after(tokens, *ready), g, gh, w, gains)
    for h in w_reduce:
        h.got = [after(p, grad_tokens) for p in h.got]
        h.reduce_two()
    grad_out = add([wo_parts[0], *wo_got])
    output = down([after(acts_o[0], grad_tokens), *acts_o[1:]], downs, [hidden, out_r])
    for h in w_reduce:
        h.got = [after(p, output) for p in h.got]
    w_parts = [jnp.concatenate(p, axis=1) for p in zip(*[h.sum_two(na) for h in w_reduce])]
    gw = add([w_parts[0], *send_on(w_parts, "f1", na)])

    sums = jnp.stack([s.reshape(shard, 2, wide) for s in sums], axis=1).reshape(shard, chunks, wide)
    grad_down = sums[:, :, model:].transpose(1, 0, 2).reshape(chunks * shard, model).astype(f32)
    g_up = sums[:, :, :model].reshape(shard, chunks, 2, part)
    keep = jnp.where(core == 0, g_up[:, :, 0], g_up[:, :, 1])
    come = swap(jnp.where(core == 0, g_up[:, :, 1], g_up[:, :, 0]))
    grad_up = jnp.where(core == 0, jnp.stack([keep, come], 0), jnp.stack([come, keep], 0))
    grad_up = grad_up.reshape(2, shard, chunks, nx, fsdp, shard).transpose(1, 3, 0, 4, 2, 5)
    grad_up = grad_up.reshape(shard, ff).astype(f32)

    qw = query_weight.shape[1]
    return (
        output,
        grad_tokens,
        gw[:, qw + 2 * HEAD],
        gw[:, :qw],
        gw[:, qw : qw + HEAD],
        gw[:, qw + HEAD : qw + 2 * HEAD],
        grad_out,
        gw[:, qw + 2 * HEAD + 1],
        grad_up,
        grad_down,
    )


def solution(mesh):
    dp, fsdp = mesh.shape["dp"], mesh.shape["fsdp"]
    sizes = (dp // 2, 4, fsdp // 4)
    names = ("x", "core", "f1", "f2")
    split = Mesh(mesh.devices.reshape(sizes[0], 2, *sizes[1:]), names)
    rows, line = P(names, None), P(names)
    return jax.shard_map(
        functools.partial(on_device, sizes),
        mesh=split,
        in_specs=(rows, rows, line, rows, rows, rows, rows, line, rows, rows, rows),
        out_specs=(rows, rows, line, rows, rows, rows, rows, line, rows, rows),
        check_vma=False,
    )
```

```python
import functools
import math

import jax
import jax.numpy as jnp
from jax import lax
from jax.experimental import pallas as pl
from jax.experimental.pallas import tpu as pltpu
from jax.sharding import Mesh, PartitionSpec as P

EPS = 1e-06
HEAD = 128
MIB = 2**20
f32 = jnp.float32
bf16 = jnp.bfloat16
VM = pl.BlockSpec(memory_space=pltpu.VMEM)
NEAR = pl.BlockSpec(memory_space=pltpu.VMEM)
SM = pl.BlockSpec(memory_space=pltpu.SMEM)
GELU_A = math.sqrt(2.0 / math.pi)
GELU_B = GELU_A * 0.044715
SCORE_SCALE = 1.0 / math.sqrt(HEAD)
LOG2E = math.log2(math.e)
MARKS = 64
GROUP = 2
VMEM_MIB = 60
HINT = 8
FFN_MIB = 44


def nn(a, b):
    return lax.dot_general(a, b, (((1,), (0,)), ((), ())), preferred_element_type=f32)


def nt(a, b):
    return lax.dot_general(a, b, (((1,), (1,)), ((), ())), preferred_element_type=f32)


def tn(a, b):
    return lax.dot_general(a, b, (((0,), (0,)), ((), ())), preferred_element_type=f32)


def shape(dims, dtype):
    return jax.ShapeDtypeStruct(dims, dtype)


def call(kernel, outs, args, flops, exps=0, scratch=(), vmem=48, name=None, in_specs=None, **kw):
    moved = sum(math.prod(a.shape) * a.dtype.itemsize for a in (*args, *outs))
    specs = in_specs or [VM] * len(args)
    args = [
        a if s is SM else pltpu.with_memory_space_constraint(a, pltpu.VMEM if s is NEAR else pltpu.HBM)
        for a, s in zip(args, specs)
    ]
    outs = [pltpu.HBM(a.shape, a.dtype) for a in outs]
    return pl.pallas_call(
        kernel,
        out_shape=outs,
        in_specs=specs,
        out_specs=kw.pop("out_specs", [VM] * len(outs)),
        scratch_shapes=list(scratch),
        compiler_params=pltpu.CompilerParams(vmem_limit_bytes=vmem * MIB),
        cost_estimate=pl.CostEstimate(flops=flops // HINT, bytes_accessed=moved // HINT, transcendentals=exps // HINT),
        name=name,
        **kw,
    )(*args)


def chip_at(sizes, order, me_ref, rx, rb, ra, sign):
    nx, na, nb = sizes
    x = lax.rem(me_ref[0] + (sign * rx) % nx, nx)
    a = lax.rem(me_ref[1] + (sign * ra) % na, na) if order[1] else ra
    b = lax.rem(me_ref[2] + (sign * rb) % nb, nb)
    return x, a * nb + b


def blocks_of(sizes, order):
    nx, na, nb = sizes
    for rx in range(nx):
        for rb in range(nb):
            for ra in range(na):
                yield (rx, rb, ra), (rx, rb) if order[0] else (rb, rx)


def seconds(sizes, order):
    return sizes[2] if order[0] else sizes[0]


def firsts(sizes, order):
    return sizes[0] if order[0] else sizes[2]


def row_of(sizes, x, f, core, shard):
    return pl.ds(pl.multiple_of(((x * 2 + core) * (sizes[1] * sizes[2]) + f) * shard, shard), shard)


def half_row_of(sizes, x, f, shard):
    return pl.ds(pl.multiple_of((x * (sizes[1] * sizes[2]) + f) * shard, shard), shard)


def assemble(sizes, me_ref, orders, refs, whole_ref):
    refs, column = list(refs), 0
    for order in orders:
        count = seconds(sizes, order)
        mine, refs = refs[: 2 * count], refs[2 * count :]
        width = mine[0].shape[1]
        shard = mine[0].shape[0] // (firsts(sizes, order) * sizes[1])
        for other in range(2):
            core = me_ref[3] if other == 0 else 1 - me_ref[3]
            for place, (first, second) in blocks_of(sizes, order):
                x, f = chip_at(sizes, order, me_ref, *place, -1)
                at = (first * sizes[1] + place[2]) * shard
                whole_ref[row_of(sizes, x, f, core, shard), column : column + width] = mine[other * count + second][at : at + shard, :]
        column += width


def hand_out(sizes, me_ref, orders, whole_ref, refs):
    nx, na, nb = sizes
    column = 0
    for n, order in enumerate(orders):
        for other, ref in enumerate(refs[2 * n : 2 * n + 2]):
            core = me_ref[3] if other == 0 else 1 - me_ref[3]
            shard = ref.shape[0] // (nx * na * nb)
            for place, (first, second) in blocks_of(sizes, order):
                x, f = chip_at(sizes, order, me_ref, *place, 1)
                at = ((first * seconds(sizes, order) + second) * na + place[2]) * shard
                ref[at : at + shard, :] = whole_ref[row_of(sizes, x, f, core, shard), column : column + ref.shape[1]]
        column += refs[2 * n].shape[1]


def gain_rows(block):
    return block.astype(f32).T


def norm_tile(x, gain):
    r = lax.rsqrt(jnp.mean(x * x, axis=-1, keepdims=True) + EPS)
    return x * r * gain


def position_ids(len_ref, pos):
    seg = jnp.zeros(pos.shape, jnp.int32)
    end = jnp.int32(0)
    slots = len_ref.shape[1]
    for slot in range(slots):
        end = end + len_ref[0, slot]
        seg = seg + (pos >= end).astype(jnp.int32)
    return jnp.where(pos >= end, slots + pos // 128, seg), pos >= end


def query_marks(len_ref, first):
    pos = first + lax.broadcasted_iota(jnp.int32, (128, 1), 0)
    ids, _ = position_ids(len_ref, pos)
    lane = lax.broadcasted_iota(jnp.int32, (128, 128), 1)
    return jnp.where(lane == ids, 1.0, 0.0)


def key_marks(len_ref, first):
    pos = first + lax.broadcasted_iota(jnp.int32, (128, 1), 0)
    ids, _ = position_ids(len_ref, pos)
    lane = lax.broadcasted_iota(jnp.int32, (128, 128), 1)
    return jnp.where(lane >= MARKS, 1.0, jnp.where(lane == ids, 0.0, -1e30)).astype(bf16)


def block_bias(len_ref, first):
    q_pos = first + lax.broadcasted_iota(jnp.int32, (128, 1), 0)
    k_pos = first + lax.broadcasted_iota(jnp.int32, (1, 128), 1)
    _, k_pad = position_ids(len_ref, k_pos)
    allowed = ((k_pos <= q_pos) & jnp.logical_not(k_pad)) | (k_pos == q_pos)
    return jnp.where(allowed, 0.0, -1e30)


def split3(v):
    hi = v.astype(bf16).astype(f32)
    mid = (v - hi).astype(bf16).astype(f32)
    return hi, mid, v - hi - mid


def at_lanes(base, first, values):
    lane = lax.broadcasted_iota(jnp.int32, base.shape, 1)
    for n, v in enumerate(values):
        base = jnp.where(lane == first + n, v, base)
    return base


def stack(a, heads):
    return jnp.concatenate([a[:, h * HEAD : (h + 1) * HEAD] for h in range(heads)], axis=0)


def project_kernel(sizes, orders, me_ref, x_ref, *refs):
    *pieces, w_ref, qkv_ref, gains_ref, normed = refs
    assemble(sizes, me_ref, orders, pieces, w_ref)
    rows = x_ref.shape[0]
    wide = qkv_ref.shape[1]
    key_at = wide - 2 * HEAD
    gains_ref[...] = gain_rows(w_ref[:, wide : wide + HEAD])[:8]

    @pl.loop(0, rows // 128, unroll=True)
    def _(t):
        at = pl.ds(pl.multiple_of(t * 128, 128), 128)
        normed[at, :] = norm_tile(x_ref[at, :].astype(f32), gains_ref[0:1, :]).astype(bf16)

    @pl.loop(0, key_at // 256, unroll=True)
    def _(j):
        at = pl.ds(pl.multiple_of(j * 256, 256), 256)
        qkv_ref[:, at] = (nn(normed[...], w_ref[:, at]) * (SCORE_SCALE * LOG2E)).astype(bf16)

    qkv_ref[:, key_at:] = nn(normed[...], w_ref[:, key_at:wide]).astype(bf16)


def project(sizes, orders, columns, me, x, pieces):
    rows, model = x.shape
    wide = columns - HEAD
    return call(
        functools.partial(project_kernel, sizes, orders),
        [shape((model, columns), bf16), shape((rows, wide), bf16), shape((8, model), f32)],
        (me, x, *pieces),
        2 * rows * model * wide,
        0,
        [pltpu.VMEM((rows, model), bf16)],
        VMEM_MIB,
        "project",
        [SM] + [VM] * (1 + len(pieces)),
    )


def marked(len_ref, qkv_ref, keys, values):
    rows, wide = qkv_ref.shape
    keys[:, :HEAD] = qkv_ref[:, wide - 2 * HEAD : wide - HEAD]
    values[:, :HEAD] = qkv_ref[:, wide - HEAD :]

    @pl.loop(0, rows // 128, unroll=True)
    def _(t):
        at = pl.ds(pl.multiple_of(t * 128, 128), 128)
        keys[at, HEAD:] = key_marks(len_ref, t * 128)
        values[at, HEAD:] = jnp.ones((128, HEAD), bf16)


def attention_forward_kernel(len_ref, qkv_ref, att_ref, lse_ref, keys, values):
    rows, wide = qkv_ref.shape
    heads = (wide - 2 * HEAD) // HEAD
    marked(len_ref, qkv_ref, keys, values)

    for i in range(rows // 128):
        ext = (i + 1) * 128
        q_at = slice(i * 128, ext)
        marks = query_marks(len_ref, i * 128).astype(bf16)
        bias = block_bias(len_ref, i * 128)
        lse = jnp.zeros((128, HEAD), f32)
        lane = lax.broadcasted_iota(jnp.int32, (128, HEAD), 1)
        for first in range(0, heads, GROUP):
            cols = slice(first * HEAD, (first + GROUP) * HEAD)
            q = stack(qkv_ref[q_at, cols], GROUP)
            q = jnp.concatenate([q, jnp.concatenate([marks] * GROUP, axis=0)], axis=1)
            s = nt(q, keys[:ext, :])
            last = s[:, ext - 128 :] + jnp.concatenate([bias] * GROUP, axis=0)
            s = jnp.concatenate([s[:, : ext - 128], last], axis=1) if i else last
            peak = jnp.max(s, axis=-1, keepdims=True)
            e = jnp.exp2(s - peak).astype(bf16)
            o = nn(e, values[:ext, :])
            total = o[:, HEAD:]
            low = peak + jnp.log2(total)
            o = (o[:, :HEAD] / total).astype(bf16)
            att_ref[q_at, cols] = jnp.concatenate([o[h * 128 : (h + 1) * 128] for h in range(GROUP)], axis=1)
            for h in range(GROUP):
                lse = jnp.where(lane == first + h, low[h * 128 : (h + 1) * 128], lse)
        lse_ref[q_at, :] = lse


def attention_forward(lengths, qkv):
    rows, wide = qkv.shape
    model = wide - 2 * HEAD
    return call(
        attention_forward_kernel,
        [shape((rows, model), bf16), shape((rows, HEAD), f32)],
        (lengths, qkv),
        4 * rows * rows * model,
        rows * rows * 4,
        [pltpu.VMEM((rows, 2 * HEAD), bf16), pltpu.VMEM((rows, 2 * HEAD), bf16)],
        VMEM_MIB,
        "attention_forward",
        [SM, VM],
    )


def branch_kernel(sizes, orders, me_ref, x_ref, att_ref, gains_ref, *refs):
    *pieces, wo_ref, hidden_ref, nt_ref = refs

    @pl.when(pl.program_id(0) == 0)
    def _():
        assemble(sizes, me_ref, orders, pieces, wo_ref)

    hidden_ref[...] = x_ref[...].astype(f32) + nn(att_ref[...], wo_ref[...])

    @pl.loop(0, x_ref.shape[0] // 128, unroll=True)
    def _(t):
        at = pl.ds(pl.multiple_of(t * 128, 128), 128)
        nt_ref[at, :] = norm_tile(hidden_ref[at, :], gains_ref[1:2, :]).astype(bf16)


def held(a):
    return pl.BlockSpec(a.shape, lambda i: (0, 0), pipeline_mode=pl.Buffered(1))


def branch(sizes, orders, me, x, att, gains, pieces):
    rows, model = x.shape
    tile = rows // 4
    wo = shape((model, model), bf16)
    strip = pl.BlockSpec((tile, model), lambda i: (i, 0))
    return call(
        functools.partial(branch_kernel, sizes, orders),
        [wo, shape((rows, model), f32), shape((rows, model), bf16)],
        (me, x, att, gains, *pieces),
        2 * rows * model * model,
        0,
        (),
        VMEM_MIB,
        "branch",
        [SM, strip, strip, held(gains), *map(held, pieces)],
        grid=(rows // tile,),
        out_specs=[held(wo), strip, strip],
    )


def gelu_both(v):
    v2 = v * v
    t = jnp.tanh(v * (GELU_A + GELU_B * v2))
    h = 0.5 + 0.5 * t
    a = v * h
    return a, h + (a - a * h) * ((2 * GELU_A) + (6 * GELU_B) * v2)


def ffn_kernel(sizes, order, me_ref, *refs):
    count, lines = seconds(sizes, order), firsts(sizes, order)
    take = lambda n: [refs.pop(0) for _ in range(n)]
    refs = list(refs)
    near, ins = take(4), take(count)
    seen, whole, outs = take(4), take(2), take(lines)
    pieces = take(count)
    acts, (up_ref, down_ref), (gu, gd), staged = take(4), take(2), take(2), take(lines)
    in_sem, out_sem = refs
    part, model = down_ref.shape
    shard = part // math.prod(sizes)
    tile = min(256, part)

    loads = [pltpu.make_async_copy(a, b, in_sem.at[n]) for n, (a, b) in enumerate(zip(ins, pieces))]
    for load in loads:
        load.start()
    started = []

    def store(src, dst):
        copy = pltpu.make_async_copy(src, dst, out_sem.at[len(started)])
        copy.start()
        started.append(copy)

    for load in loads:
        load.wait()
    for place, (first, second) in blocks_of(sizes, order):
        x, f = chip_at(sizes, order, me_ref, *place, -1)
        row = (first * sizes[1] + place[2]) * shard
        at = slice(row, row + shard)
        for core in range(2):
            up_ref[row_of(sizes, x, f, core, shard), :] = pieces[second][at, core * part : (core + 1) * part]
        down_ref[half_row_of(sizes, x, f, shard), :] = pieces[second][at, 2 * part :]

    nt_o, nt_p, dy_o, dy_p = near
    act_o, act_p, gi_o, gi_p = acts
    tiles = [slice(j * tile, (j + 1) * tile) for j in range(part // tile)]
    for j, cols in enumerate(tiles):
        for own, (n_ref, y_ref, a_ref, i_ref) in enumerate(((nt_o, dy_o, act_o, gi_o), (nt_p, dy_p, act_p, gi_p))):
            inner = nn(n_ref[...], up_ref[:, cols])
            ga = nt(y_ref[...], down_ref[cols, :])
            a, slope = gelu_both(inner)
            a_ref[:, cols] = a.astype(bf16)
            i_ref[:, cols] = (ga * slope).astype(bf16)
            if j == len(tiles) - 1:
                store(a_ref, seen[own])
                store(i_ref, seen[2 + own])
    store(up_ref, whole[0])
    store(down_ref, whole[1])
    for cols in tiles:
        gu[:, cols] = (tn(nt_o[...], gi_o[:, cols]) + tn(nt_p[...], gi_p[:, cols])).astype(bf16)
    for cols in tiles:
        gd[cols, :] = (tn(act_o[:, cols], dy_o[...]) + tn(act_p[:, cols], dy_p[...])).astype(bf16)

    for line in reversed(range(lines)):
        for place, (first, second) in blocks_of(sizes, order):
            if first != line:
                continue
            x, f = chip_at(sizes, order, me_ref, *place, 1)
            row = (second * sizes[1] + place[2]) * shard
            at = slice(row, row + shard)
            for core in range(2):
                staged[line][at, core * part : (core + 1) * part] = gu[row_of(sizes, x, f, core, shard), :]
            staged[line][at, 2 * part :] = gd[half_row_of(sizes, x, f, shard), :]
        store(staged[line], outs[line])
    for copy in started:
        copy.wait()


def ffn(sizes, order, me, nt_o, nt_p, dy_o, dy_p, pieces):
    rows, model = nt_o.shape
    part = model // 2
    up, down = shape((model, part), bf16), shape((part, model), bf16)
    lines = firsts(sizes, order)
    grads = [shape((part // lines, 2 * model), bf16)] * lines
    ins = (nt_o, nt_p, dy_o, dy_p, *pieces)
    outs = [shape((rows, part), bf16)] * 4 + [up, down] + grads
    far = pl.BlockSpec(memory_space=pltpu.HBM)
    outs = call(
        functools.partial(ffn_kernel, sizes, order),
        outs,
        (me, *ins),
        16 * rows * model * part,
        2 * rows * part,
        [pltpu.VMEM(a.shape, bf16) for a in (*pieces, *outs[:4], up, down, up, down, *grads)]
        + [pltpu.SemaphoreType.DMA((len(pieces),)), pltpu.SemaphoreType.DMA((len(outs),))],
        FFN_MIB,
        "ffn",
        [SM] + [NEAR] * 4 + [far] * len(pieces),
        out_specs=[far] * len(outs),
    )
    return outs[:4], outs[4], outs[5], outs[6:]


def hidden_backward_kernel(count, *refs):
    gis, ups, gn_ref = refs[:count], refs[count : 2 * count], refs[2 * count]
    total = None
    for i, u in zip(gis, ups):
        v = nt(i[...], u[...])
        total = v if total is None else total + v
    gn_ref[...] = total.astype(bf16)


def hidden_backward(gis, ups):
    rows, part = gis[0].shape
    model = ups[0].shape[0]
    count = len(gis)
    tile = model // 4
    return call(
        functools.partial(hidden_backward_kernel, count),
        [shape((rows, model), bf16)],
        (*gis, *ups),
        count * 2 * rows * part * model,
        0,
        (),
        VMEM_MIB,
        "hidden_backward",
        [pl.BlockSpec((tile, part), lambda g: (g, 0))] * count + [held(u) for u in ups],
        grid=(rows // tile,),
        out_specs=[pl.BlockSpec((tile, model), lambda g: (g, 0))],
    )[0]


def down_kernel(count, *refs):
    acts, downs, more, out_ref = refs[:count], refs[count : 2 * count], refs[2 * count : -1], refs[-1]
    total = None
    for a, d in zip(acts, downs):
        v = nn(a[...], d[...])
        total = v if total is None else total + v
    for m in more:
        total = total + m[...].astype(f32)
    out_ref[...] = total.astype(bf16)


def down(acts, downs, more):
    rows, part = acts[0].shape
    model = downs[0].shape[1]
    count = len(acts)
    tile = rows // 4
    strip = pl.BlockSpec((tile, model), lambda g: (g, 0))
    return call(
        functools.partial(down_kernel, count),
        [shape((rows, model), bf16)],
        (*acts, *downs, *more),
        count * 2 * rows * part * model,
        0,
        (),
        VMEM_MIB,
        "down",
        [pl.BlockSpec((tile, part), lambda g: (g, 0))] * count + [held(d) for d in downs] + [strip] * len(more),
        grid=(rows // tile,),
        out_specs=[strip],
    )[0]


def branch_backward_kernel(sizes, orders, count, me_ref, hidden_ref, gn_ref, dy_ref, att_ref, gains_ref, wo_ref, *refs):
    gis, ups, refs = refs[:count], refs[count : 2 * count], refs[2 * count :]
    gh_ref, gatt_ref, gg_ref, *halves, gn, gb, gwo, low = refs
    step = pl.program_id(0)
    rows = hidden_ref.shape[0]

    @pl.when(step == 0)
    def _():
        gg_ref[...] = jnp.zeros_like(gg_ref)
        gwo[...] = jnp.zeros_like(gwo)

    total = gn_ref[...].astype(f32)
    for i, u in zip(gis, ups):
        total = total + nt(i[...], u[...])
    gn[...] = total

    @pl.loop(0, rows // 64, unroll=True)
    def _(t):
        at = pl.ds(pl.multiple_of(t * 64, 64), 64)
        h, n = hidden_ref[at, :], gn[at, :]
        r = lax.rsqrt(jnp.mean(h * h, axis=-1, keepdims=True) + EPS)
        z = h * r
        gg_ref[1:2, :] += jnp.sum(n * z, axis=0, keepdims=True)
        g = n * gains_ref[1:2, :]
        gh = dy_ref[at, :].astype(f32) + r * (g - z * jnp.mean(g * z, axis=-1, keepdims=True))
        gh_ref[at, :] = gh
        gb[at, :] = gh.astype(bf16)

    gatt_ref[...] = nt(gb[...], wo_ref[...]).astype(bf16)
    gwo[...] += tn(att_ref[...], gb[...])

    @pl.when(step == pl.num_programs(0) - 1)
    def _():
        low[...] = gwo[...].astype(bf16)
        hand_out(sizes, me_ref, orders, low, halves)


def branch_backward(sizes, orders, me, hidden, gn, dy, att, gains, wo, gis, ups):
    rows, model = hidden.shape
    part = gis[0].shape[1]
    count = len(gis)
    tile = rows // 4
    strip = pl.BlockSpec((tile, model), lambda i: (i, 0))
    gg = shape((8, model), f32)
    halves = [shape((model // 2, model // len(orders)), bf16)] * (2 * len(orders))
    return call(
        functools.partial(branch_backward_kernel, sizes, orders, count),
        [shape((rows, model), f32), shape((rows, model), bf16), gg, *halves],
        (me, hidden, gn, dy, att, gains, wo, *gis, *ups),
        4 * rows * model * model + count * 2 * rows * part * model,
        0,
        [
            pltpu.VMEM((tile, model), f32),
            pltpu.VMEM((tile, model), bf16),
            pltpu.VMEM((model, model), f32),
            pltpu.VMEM((model, model), bf16),
        ],
        VMEM_MIB,
        "branch_backward",
        [SM, strip, strip, strip, strip, held(gains), held(wo)]
        + [pl.BlockSpec((tile, part), lambda i: (i, 0))] * count
        + [held(u) for u in ups],
        grid=(rows // tile,),
        out_specs=[strip, strip, held(gg), *map(held, halves)],
    )


def attention_backward_kernel(
    len_ref, qkv_ref, ga_ref, att_ref, lse_ref, g_ref, keys, values, probs, gscores, dk, dv
):
    rows, wide = qkv_ref.shape
    heads = (wide - 2 * HEAD) // HEAD
    key_at = heads * HEAD
    dk[...] = jnp.zeros_like(dk)
    dv[...] = jnp.zeros_like(dv)
    marked(len_ref, qkv_ref, keys, values)

    for i in range(rows // 128):
        ext = (i + 1) * 128
        q_at = slice(i * 128, ext)
        marks = query_marks(len_ref, i * 128)
        bias = block_bias(len_ref, i * 128)
        for first in range(0, heads, GROUP):
            cols = slice(first * HEAD, (first + GROUP) * HEAD)
            q = stack(qkv_ref[q_at, cols], GROUP)
            ga = stack(ga_ref[q_at, cols], GROUP)
            q_more, ga_more = [], []
            for h in range(first, first + GROUP):
                at = slice(h * HEAD, (h + 1) * HEAD)
                q_more.append(at_lanes(marks, MARKS, split3(-lse_ref[q_at, h : h + 1])).astype(bf16))
                delta = jnp.sum(ga_ref[q_at, at].astype(f32) * att_ref[q_at, at].astype(f32), axis=-1, keepdims=True)
                ga_more.append(at_lanes(jnp.zeros((128, HEAD), f32), 0, split3(-delta)).astype(bf16))
            s = nt(jnp.concatenate([q, jnp.concatenate(q_more, axis=0)], axis=1), keys[:ext, :])
            gp = nt(jnp.concatenate([ga, jnp.concatenate(ga_more, axis=0)], axis=1), values[:ext, :])
            last = s[:, ext - 128 :] + jnp.concatenate([bias] * GROUP, axis=0)
            s = jnp.concatenate([s[:, : ext - 128], last], axis=1) if i else last
            p = jnp.exp2(s)
            out = slice(first * 128, (first + GROUP) * 128)
            probs[out, :ext] = p.astype(bf16)
            gscores[out, :ext] = (p * gp).astype(bf16)
        dv[:ext, :] += tn(probs[:, :ext], stack(ga_ref[q_at, :], heads))
        dk[:ext, :] += tn(gscores[:, :ext], stack(qkv_ref[q_at, :key_at], heads))
        gq = (nn(gscores[:, :ext], keys[:ext, :HEAD]) * SCORE_SCALE).astype(bf16)
        g_ref[q_at, :key_at] = jnp.concatenate([gq[h * 128 : (h + 1) * 128] for h in range(heads)], axis=1)

    g_ref[:, key_at : key_at + HEAD] = (dk[...] * (1.0 / LOG2E)).astype(bf16)
    g_ref[:, key_at + HEAD :] = dv[...].astype(bf16)


def attention_backward(lengths, qkv, ga, att, lse):
    rows, wide = qkv.shape
    model = ga.shape[1]
    return call(
        attention_backward_kernel,
        [shape(qkv.shape, bf16)],
        (lengths, qkv, ga, att, lse),
        10 * rows * rows * model,
        rows * rows * 4,
        [
            pltpu.VMEM((rows, 2 * HEAD), bf16),
            pltpu.VMEM((rows, 2 * HEAD), bf16),
            pltpu.VMEM((model, rows), bf16),
            pltpu.VMEM((model, rows), bf16),
            pltpu.VMEM((rows, HEAD), f32),
            pltpu.VMEM((rows, HEAD), f32),
        ],
        VMEM_MIB,
        "attention_backward",
        [SM] + [VM] * 4,
    )[0]


def projection_grads_kernel(sizes, orders, me_ref, x_ref, g_ref, w_ref, gains_ref, gg_ref, *refs):
    *halves, normed, gw = refs
    rows, model = x_ref.shape
    wide = g_ref.shape[1]

    @pl.loop(0, rows // 128, unroll=True)
    def _(t):
        at = pl.ds(pl.multiple_of(t * 128, 128), 128)
        normed[at, :] = norm_tile(x_ref[at, :].astype(f32), gains_ref[0:1, :]).astype(bf16)

    dots = jnp.zeros((model, HEAD), f32)
    for j in range(wide // 256):
        at = slice(j * 256, (j + 1) * 256)
        v = tn(normed[...], g_ref[:, at])
        gw[:, at] = v.astype(bf16)
        v = v * w_ref[:, at].astype(f32)
        dots = dots + (v[:, :HEAD] + v[:, HEAD:])
    one = jnp.sum(dots, axis=-1, keepdims=True) / w_ref[:, wide : wide + 1].astype(f32)
    two = jnp.concatenate([gg_ref[...], jnp.zeros((HEAD - 8, model), f32)], axis=0).T
    lane = lax.broadcasted_iota(jnp.int32, (model, HEAD), 1)
    gw[:, wide : wide + HEAD] = jnp.where(lane == 0, one, two).astype(bf16)
    hand_out(sizes, me_ref, orders, gw, halves)


def projection_grads(sizes, orders, widths, me, x, g, w, gains, gg):
    rows, model = x.shape
    halves = [shape((w.shape[0] // 2, width), bf16) for width in widths for _ in range(2)]
    return call(
        functools.partial(projection_grads_kernel, sizes, orders),
        halves,
        (me, x, g, w, gains, gg),
        2 * rows * model * g.shape[1],
        0,
        [pltpu.VMEM((rows, model), bf16), pltpu.VMEM(w.shape, bf16)],
        VMEM_MIB,
        "projection_grads",
        [SM] + [VM] * 5,
    )


def input_backward_kernel(x_ref, g_ref, gh_ref, w_ref, gains_ref, gx_ref, gn):
    rows = x_ref.shape[0]
    gn[...] = nt(g_ref[...], w_ref[:, : g_ref.shape[1]])

    @pl.loop(0, rows // 64, unroll=True)
    def _(t):
        at = pl.ds(pl.multiple_of(t * 64, 64), 64)
        x = x_ref[at, :].astype(f32)
        r = lax.rsqrt(jnp.mean(x * x, axis=-1, keepdims=True) + EPS)
        z = x * r
        g = gn[at, :] * gains_ref[0:1, :]
        gx_ref[at, :] = (gh_ref[at, :] + r * (g - z * jnp.mean(g * z, axis=-1, keepdims=True))).astype(bf16)


def input_backward(x, g, gh, w, gains):
    rows, model = x.shape
    tile = rows // 4
    strip = lambda a: pl.BlockSpec((tile, a.shape[1]), lambda i: (i, 0))
    return call(
        input_backward_kernel,
        [shape(x.shape, bf16)],
        (x, g, gh, w, gains),
        2 * rows * model * g.shape[1],
        0,
        [pltpu.VMEM((tile, model), f32)],
        VMEM_MIB,
        "input_backward",
        [strip(x), strip(g), strip(gh), held(w), held(gains)],
        grid=(rows // tile,),
        out_specs=[strip(x)],
    )[0]


def after(a, *first):
    return lax.optimization_barrier((a, *first))[0]


def spread(a, axis, n):
    return [a] + [lax.ppermute(a, axis, [(i, (i + s) % n) for i in range(n)]) for s in range(1, n)]


def add(parts):
    total = parts[0].astype(f32)
    for p in parts[1:]:
        total = total + p.astype(f32)
    return total


def send_on(parts, axis, n):
    return [lax.ppermute(parts[s], axis, [(i, (i + s) % n) for i in range(n)]) for s in range(1, n)]


def cut(a, s, n):
    rows = a.shape[0] // n
    return a[s * rows : (s + 1) * rows]


def cut_columns(a, s, n):
    columns = a.shape[1] // n
    return a[:, s * columns : (s + 1) * columns]


class Hops:
    def __init__(self, sizes, order):
        x, b = ("x", sizes[0]), ("f2", sizes[2])
        self.axes = (x, b) if order[0] else (b, x)

    def gather_one(self, block):
        self.lines = spread(block, *self.axes[0])
        return self.lines[1:]

    def gather_two(self):
        self.pieces = spread(jnp.concatenate(self.lines, axis=0), *self.axes[1])
        return self.pieces

    def reduce_one(self, parts):
        self.got = [parts[0], *send_on(parts, *self.axes[0])]

    def hold(self, *first):
        self.got[1:] = [after(p, *first) for p in self.got[1:]]

    def reduce_two(self):
        n = self.axes[1][1]
        parts = [add([cut(p, s, n) for p in self.got]).astype(bf16) for s in range(n)]
        self.got = [parts[0], *send_on(parts, *self.axes[1])]
        return parts

    def sum_two(self, n=1):
        return [add([cut(p, s, n) for p in self.got]).astype(bf16) for s in range(n)]


def on_device(
    sizes, tokens, doc_lengths, gain_one, query_weight, key_weight, value_weight, out_weight,
    gain_two, up_weight, down_weight, cotangent,
):
    nx, na, nb = sizes
    fsdp = na * nb
    core = lax.axis_index("core")
    me = jnp.stack([lax.axis_index(a) for a in ("x", "f1", "f2", "core")]).astype(jnp.int32)
    swap = lambda a: lax.ppermute(a, "core", [(0, 1), (1, 0)])
    rows, model = tokens.shape
    shard = query_weight.shape[0]
    ff = up_weight.shape[1]
    chunks = down_weight.shape[0] // shard
    part = ff // (2 * chunks)
    wide = 2 * model
    x_then, b_then = (True, True), (False, True)
    by_index = [(c % 2 == 0, False) for c in range(chunks)]

    lane = lax.broadcasted_iota(jnp.int32, (shard, HEAD), 1)
    gain_block = jnp.where(lane == 0, gain_one[:, None], jnp.where(lane == 1, gain_two[:, None], jnp.zeros((), bf16)))
    w_rows = jnp.concatenate([query_weight, key_weight, value_weight, gain_block], axis=1)
    columns = w_rows.shape[1]
    first_share = columns // 256 * HEAD
    w_orders, w_widths = (x_then, b_then), (first_share, columns - first_share)
    w_along = spread(w_rows, "f1", na)

    up = up_weight.reshape(shard, nx, 2, fsdp, chunks, shard).transpose(2, 0, 4, 1, 3, 5)
    up = up.reshape(2, shard, chunks, part)
    up_keep = jnp.where(core == 0, up[0], up[1])
    up_come = swap(jnp.where(core == 0, up[1], up[0]))
    up_pair = jnp.where(core == 0, jnp.stack([up_keep, up_come], 2), jnp.stack([up_come, up_keep], 2))
    up_pair = up_pair.reshape(shard, chunks, wide // 2)
    down_rows = down_weight.reshape(chunks, shard, model)
    f_along = []
    for first in range(0, chunks, 2):
        mine = [p for c in (first, first + 1) for p in (up_pair[:, c], down_rows[c])]
        mine = jnp.concatenate(mine + ([] if first else [out_weight]), axis=1)
        f_along.append(lax.all_gather(after(mine, *w_along[1:]), "f1", axis=0, tiled=True))

    dy_p = swap(after(cotangent, *w_along[1:]))
    w_block = jnp.concatenate(w_along, axis=0)
    w_hops = [Hops(sizes, order) for order in w_orders]
    lines = w_hops[0].gather_one(w_block[:, :first_share]) + w_hops[1].gather_one(w_block[:, first_share:])
    w_pieces = []
    for h in w_hops:
        p = h.gather_two()
        w_pieces += p + [swap(a) for a in p]
    wo_orders, wo_back = ((True, False), (False, False)), (x_then,)
    hops = [Hops(sizes, order) for order in by_index]
    f_lines = lambda c: hops[c].gather_one(cut_columns(f_along[c // 2], c % 2, 2))

    w, qkv, gains = project(sizes, w_orders, columns, me, tokens, w_pieces)
    f_along[0] = after(f_along[0], qkv)
    wo_block, f_along[0] = f_along[0][:, 2 * wide :], f_along[0][:, : 2 * wide]
    wo_hops = [Hops(sizes, order) for order in wo_orders]
    for n, h in enumerate(wo_hops):
        h.gather_one(cut_columns(wo_block, n, 2))
    lines = [p for c in (0, 1) for p in f_lines(c)]
    att, lse = attention_forward(doc_lengths, after(qkv, dy_p))
    for h in wo_hops:
        h.lines[1:] = [after(p, att) for p in h.lines[1:]]
    wo_pieces = [h.gather_two() for h in wo_hops]
    wo_pieces = [a for p in wo_pieces for a in (*p, *[swap(b) for b in p])]
    for c in (0, 1):
        hops[c].lines[1:] = [after(p, att, *[h.pieces[1] for h in wo_hops]) for p in hops[c].lines[1:]]
    pieces = {c: hops[c].gather_two() for c in (0, 1)}
    wo, hidden, nt_o = branch(sizes, wo_orders, me, tokens, att, gains, wo_pieces)
    nt_o = after(nt_o, *pieces[0], *pieces[1], f_along[1])
    nt_p = swap(nt_o)

    acts_o, acts_p, gis_o, gis_p, ups, downs = [], [], [], [], [], []

    def run_ffn(c, *first):
        seen, up_c, down_c, grads = ffn(sizes, by_index[c], me, after(nt_o, *first), nt_p, cotangent, dy_p, pieces[c])
        for kept, a in zip((acts_o, acts_p, gis_o, gis_p), seen):
            kept.append(a)
        ups.append(up_c)
        downs.append(down_c)
        return grads

    def sum_cores(keep, come, order):
        n = firsts(sizes, order)
        return [add([cut(a, s, n) for a in (keep, come)]).astype(bf16) for s in range(n)]

    f_along[1] = after(f_along[1], nt_p)
    lines = [p for c in (2, 3) for p in f_lines(c)]
    grads = [run_ffn(0)]
    grads.append(run_ffn(1, *lines, ups[0]))
    for c in (2, 3):
        hops[c].lines[1:] = [after(p, ups[0]) for p in hops[c].lines[1:]]
        pieces[c] = hops[c].gather_two()
    late = [*pieces[2], *pieces[3], ups[1]]
    grads.append(run_ffn(2, *late))
    for c in (0, 1):
        hops[c].reduce_one([after(g, *late) for g in grads[c]])
    grads.append(run_ffn(3, ups[2]))
    for c in (0, 1):
        hops[c].hold(ups[3])
    ready = [p for c in (0, 1) for p in hops[c].reduce_two()]
    for c in (2, 3):
        hops[c].reduce_one([after(g, *ready) for g in grads[c]])
    gn_p = hidden_backward([after(gis_p[0], *ready), *gis_p[1:]], ups)
    gn_r = swap(gn_p)
    out_p = down([after(acts_p[0], gn_p), *acts_p[1:]], downs, [])
    last = lambda a: lax.psum_scatter(a, "f1", scatter_dimension=0, tiled=True)
    for c in (0, 1):
        hops[c].hold(out_p)
    pair = jnp.concatenate([hops[c].sum_two()[0] for c in (0, 1)], axis=1)
    sums = [last(pair)]
    gh, gatt, gg, *halves = branch_backward(
        sizes, wo_back, me, hidden, gn_r, cotangent, att, gains, wo, [after(gis_o[0], pair), *gis_o[1:]], ups
    )
    for c in (2, 3):
        hops[c].hold(gatt)
    ready = [p for c in (2, 3) for p in hops[c].reduce_two()]
    come = swap(after(halves[1], *ready))
    wo_reduce = Hops(sizes, x_then)
    ready = sum_cores(halves[0], come, x_then)
    wo_reduce.reduce_one(ready)
    g = attention_backward(doc_lengths, after(qkv, *ready), gatt, att, lse)
    for h in (hops[2], hops[3], wo_reduce):
        h.hold(g)
    pair = jnp.concatenate([hops[c].sum_two()[0] for c in (2, 3)], axis=1)
    sums.append(last(pair))
    ready = wo_reduce.reduce_two()
    out_r = swap(after(out_p, g))
    halves = projection_grads(sizes, w_orders, w_widths, me, after(tokens, *ready, pair), g, w, gains, gg)
    wo_reduce.hold(halves[0])
    wo_last = wo_reduce.sum_two()[0]
    come = [swap(after(h, wo_last)) for h in halves[1::2]]
    ready = [sum_cores(k, c, o) for k, c, o in zip(halves[0::2], come, w_orders)]
    w_reduce = [Hops(sizes, order) for order in w_orders]
    for h, r in zip(w_reduce, ready):
        h.reduce_one(r)
    ready = [r for rs in ready for r in rs]
    grad_tokens = input_backward(after(tokens, *ready), g, gh, w, gains)
    ready = []
    for h in w_reduce:
        h.hold(grad_tokens)
        ready += h.reduce_two()
    output = down([after(acts_o[0], *ready), *acts_o[1:]], downs, [hidden, out_r])
    for h in w_reduce:
        h.hold(output)
    w_parts = [jnp.concatenate([*p, cut(wo_last, n, na)], axis=1) for n, p in enumerate(zip(*[h.sum_two(na) for h in w_reduce]))]
    got = send_on(w_parts, "f1", na)

    sums = [after(a, *w_parts) for a in sums]
    sums = jnp.stack([a.reshape(shard, 2, wide) for a in sums], axis=1).reshape(shard, chunks, wide)
    grad_down = sums[:, :, model:].transpose(1, 0, 2).reshape(chunks * shard, model).astype(f32)
    g_up = sums[:, :, :model].reshape(shard, chunks, 2, part)
    keep = jnp.where(core == 0, g_up[:, :, 0], g_up[:, :, 1])
    come = swap(jnp.where(core == 0, g_up[:, :, 1], g_up[:, :, 0]))
    grad_up = jnp.where(core == 0, jnp.stack([keep, come], 0), jnp.stack([come, keep], 0))
    grad_up = grad_up.reshape(2, shard, chunks, nx, fsdp, shard).transpose(1, 3, 0, 4, 2, 5)
    grad_up = grad_up.reshape(shard, ff).astype(f32)
    gw = add([w_parts[0], *got])
    grad_out = gw[:, columns:]

    qw = query_weight.shape[1]
    return (
        output,
        grad_tokens,
        gw[:, qw + 2 * HEAD],
        gw[:, :qw],
        gw[:, qw : qw + HEAD],
        gw[:, qw + HEAD : qw + 2 * HEAD],
        grad_out,
        gw[:, qw + 2 * HEAD + 1],
        grad_up,
        grad_down,
    )


def solution(mesh):
    dp, fsdp = mesh.shape["dp"], mesh.shape["fsdp"]
    sizes = (dp // 2, 4, fsdp // 4)
    names = ("x", "core", "f1", "f2")
    split = Mesh(mesh.devices.reshape(sizes[0], 2, *sizes[1:]), names)
    rows, line = P(names, None), P(names)
    return jax.shard_map(
        functools.partial(on_device, sizes),
        mesh=split,
        in_specs=(rows, rows, line, rows, rows, rows, rows, line, rows, rows, rows),
        out_specs=(rows, rows, line, rows, rows, rows, rows, line, rows, rows),
        check_vma=False,
    )
```

```python
import functools
import math

import jax
import jax.numpy as jnp
from jax import lax
from jax.experimental import pallas as pl
from jax.experimental.pallas import tpu as pltpu
from jax.sharding import Mesh, PartitionSpec as P

EPS = 1e-06
HEAD = 128
MIB = 2**20
f32 = jnp.float32
bf16 = jnp.bfloat16
VM = pl.BlockSpec(memory_space=pltpu.VMEM)
NEAR = pl.BlockSpec(memory_space=pltpu.VMEM)
SM = pl.BlockSpec(memory_space=pltpu.SMEM)
GELU_A = math.sqrt(2.0 / math.pi)
GELU_B = GELU_A * 0.044715
SCORE_SCALE = 1.0 / math.sqrt(HEAD)
LOG2E = math.log2(math.e)
MARKS = 64
GROUP = 2
VMEM_MIB = 40
HINT = 8
FFN_MIB = 44


def nn(a, b):
    return lax.dot_general(a, b, (((1,), (0,)), ((), ())), preferred_element_type=f32)


def nt(a, b):
    return lax.dot_general(a, b, (((1,), (1,)), ((), ())), preferred_element_type=f32)


def tn(a, b):
    return lax.dot_general(a, b, (((0,), (0,)), ((), ())), preferred_element_type=f32)


def shape(dims, dtype):
    return jax.ShapeDtypeStruct(dims, dtype)


def call(kernel, outs, args, flops, exps=0, scratch=(), vmem=48, name=None, in_specs=None, **kw):
    moved = sum(math.prod(a.shape) * a.dtype.itemsize for a in (*args, *outs))
    specs = in_specs or [VM] * len(args)
    args = [
        a if s is SM else pltpu.with_memory_space_constraint(a, pltpu.VMEM if s is NEAR else pltpu.HBM)
        for a, s in zip(args, specs)
    ]
    outs = [pltpu.HBM(a.shape, a.dtype) for a in outs]
    return pl.pallas_call(
        kernel,
        out_shape=outs,
        in_specs=specs,
        out_specs=kw.pop("out_specs", [VM] * len(outs)),
        scratch_shapes=list(scratch),
        compiler_params=pltpu.CompilerParams(vmem_limit_bytes=vmem * MIB),
        cost_estimate=pl.CostEstimate(flops=flops // HINT, bytes_accessed=moved // HINT, transcendentals=exps // HINT),
        name=name,
        **kw,
    )(*args)


def chip_at(sizes, order, me_ref, rx, rb, ra, sign):
    nx, na, nb = sizes
    x = lax.rem(me_ref[0] + (sign * rx) % nx, nx)
    a = lax.rem(me_ref[1] + (sign * ra) % na, na) if order[1] else ra
    b = lax.rem(me_ref[2] + (sign * rb) % nb, nb)
    return x, a * nb + b


def blocks_of(sizes, order):
    nx, na, nb = sizes
    for rx in range(nx):
        for rb in range(nb):
            for ra in range(na):
                yield (rx, rb, ra), (rx, rb) if order[0] else (rb, rx)


def seconds(sizes, order):
    return sizes[2] if order[0] else sizes[0]


def firsts(sizes, order):
    return sizes[0] if order[0] else sizes[2]


def row_of(sizes, x, f, core, shard):
    return pl.ds(pl.multiple_of(((x * 2 + core) * (sizes[1] * sizes[2]) + f) * shard, shard), shard)


def half_row_of(sizes, x, f, shard):
    return pl.ds(pl.multiple_of((x * (sizes[1] * sizes[2]) + f) * shard, shard), shard)


def assemble(sizes, me_ref, orders, refs, whole_ref):
    refs, column = list(refs), 0
    for order in orders:
        count = seconds(sizes, order)
        mine, refs = refs[: 2 * count], refs[2 * count :]
        width = mine[0].shape[1]
        shard = mine[0].shape[0] // (firsts(sizes, order) * sizes[1])
        for other in range(2):
            core = me_ref[3] if other == 0 else 1 - me_ref[3]
            for place, (first, second) in blocks_of(sizes, order):
                x, f = chip_at(sizes, order, me_ref, *place, -1)
                at = (first * sizes[1] + place[2]) * shard
                whole_ref[row_of(sizes, x, f, core, shard), column : column + width] = mine[other * count + second][at : at + shard, :]
        column += width


def hand_out(sizes, me_ref, orders, whole_ref, refs):
    nx, na, nb = sizes
    column = 0
    for n, order in enumerate(orders):
        for other, ref in enumerate(refs[2 * n : 2 * n + 2]):
            core = me_ref[3] if other == 0 else 1 - me_ref[3]
            shard = ref.shape[0] // (nx * na * nb)
            for place, (first, second) in blocks_of(sizes, order):
                x, f = chip_at(sizes, order, me_ref, *place, 1)
                at = ((first * seconds(sizes, order) + second) * na + place[2]) * shard
                ref[at : at + shard, :] = whole_ref[row_of(sizes, x, f, core, shard), column : column + ref.shape[1]]
        column += refs[2 * n].shape[1]


def gain_rows(block):
    return block.astype(f32).T


def norm_tile(x, gain):
    r = lax.rsqrt(jnp.mean(x * x, axis=-1, keepdims=True) + EPS)
    return x * r * gain


def position_ids(len_ref, pos):
    seg = jnp.zeros(pos.shape, jnp.int32)
    end = jnp.int32(0)
    slots = len_ref.shape[1]
    for slot in range(slots):
        end = end + len_ref[0, slot]
        seg = seg + (pos >= end).astype(jnp.int32)
    return jnp.where(pos >= end, slots + pos // 128, seg), pos >= end


def query_marks(len_ref, first):
    pos = first + lax.broadcasted_iota(jnp.int32, (128, 1), 0)
    ids, _ = position_ids(len_ref, pos)
    lane = lax.broadcasted_iota(jnp.int32, (128, 128), 1)
    return jnp.where(lane == ids, 1.0, 0.0)


def key_marks(len_ref, first):
    pos = first + lax.broadcasted_iota(jnp.int32, (128, 1), 0)
    ids, _ = position_ids(len_ref, pos)
    lane = lax.broadcasted_iota(jnp.int32, (128, 128), 1)
    return jnp.where(lane >= MARKS, 1.0, jnp.where(lane == ids, 0.0, -1e30)).astype(bf16)


def block_bias(len_ref, first):
    q_pos = first + lax.broadcasted_iota(jnp.int32, (128, 1), 0)
    k_pos = first + lax.broadcasted_iota(jnp.int32, (1, 128), 1)
    _, k_pad = position_ids(len_ref, k_pos)
    allowed = ((k_pos <= q_pos) & jnp.logical_not(k_pad)) | (k_pos == q_pos)
    return jnp.where(allowed, 0.0, -1e30)


def split3(v):
    hi = v.astype(bf16).astype(f32)
    mid = (v - hi).astype(bf16).astype(f32)
    return hi, mid, v - hi - mid


def at_lanes(base, first, values):
    lane = lax.broadcasted_iota(jnp.int32, base.shape, 1)
    for n, v in enumerate(values):
        base = jnp.where(lane == first + n, v, base)
    return base


def stack(a, heads):
    return jnp.concatenate([a[:, h * HEAD : (h + 1) * HEAD] for h in range(heads)], axis=0)


def project_kernel(sizes, orders, me_ref, x_ref, *refs):
    *pieces, w_ref, qkv_ref, gains_ref, normed = refs
    assemble(sizes, me_ref, orders, pieces, w_ref)
    rows = x_ref.shape[0]
    wide = qkv_ref.shape[1]
    key_at = wide - 2 * HEAD
    gains_ref[...] = gain_rows(w_ref[:, wide : wide + HEAD])[:8]

    @pl.loop(0, rows // 128, unroll=True)
    def _(t):
        at = pl.ds(pl.multiple_of(t * 128, 128), 128)
        normed[at, :] = norm_tile(x_ref[at, :].astype(f32), gains_ref[0:1, :]).astype(bf16)

    @pl.loop(0, key_at // 256, unroll=True)
    def _(j):
        at = pl.ds(pl.multiple_of(j * 256, 256), 256)
        qkv_ref[:, at] = (nn(normed[...], w_ref[:, at]) * (SCORE_SCALE * LOG2E)).astype(bf16)

    qkv_ref[:, key_at:] = nn(normed[...], w_ref[:, key_at:wide]).astype(bf16)


def project(sizes, orders, columns, me, x, pieces):
    rows, model = x.shape
    wide = columns - HEAD
    return call(
        functools.partial(project_kernel, sizes, orders),
        [shape((model, columns), bf16), shape((rows, wide), bf16), shape((8, model), f32)],
        (me, x, *pieces),
        2 * rows * model * wide,
        0,
        [pltpu.VMEM((rows, model), bf16)],
        VMEM_MIB,
        "project",
        [SM] + [VM] * (1 + len(pieces)),
    )


def marked(len_ref, qkv_ref, keys, values):
    rows, wide = qkv_ref.shape
    keys[:, :HEAD] = qkv_ref[:, wide - 2 * HEAD : wide - HEAD]
    values[:, :HEAD] = qkv_ref[:, wide - HEAD :]

    @pl.loop(0, rows // 128, unroll=True)
    def _(t):
        at = pl.ds(pl.multiple_of(t * 128, 128), 128)
        keys[at, HEAD:] = key_marks(len_ref, t * 128)
        values[at, HEAD:] = jnp.ones((128, HEAD), bf16)


def attention_forward_kernel(len_ref, qkv_ref, att_ref, lse_ref, keys, values):
    rows, wide = qkv_ref.shape
    heads = (wide - 2 * HEAD) // HEAD
    marked(len_ref, qkv_ref, keys, values)

    for i in range(rows // 128):
        ext = (i + 1) * 128
        q_at = slice(i * 128, ext)
        marks = query_marks(len_ref, i * 128).astype(bf16)
        bias = block_bias(len_ref, i * 128)
        lse = jnp.zeros((128, HEAD), f32)
        lane = lax.broadcasted_iota(jnp.int32, (128, HEAD), 1)
        for first in range(0, heads, GROUP):
            cols = slice(first * HEAD, (first + GROUP) * HEAD)
            q = stack(qkv_ref[q_at, cols], GROUP)
            q = jnp.concatenate([q, jnp.concatenate([marks] * GROUP, axis=0)], axis=1)
            s = nt(q, keys[:ext, :])
            last = s[:, ext - 128 :] + jnp.concatenate([bias] * GROUP, axis=0)
            s = jnp.concatenate([s[:, : ext - 128], last], axis=1) if i else last
            peak = jnp.max(s, axis=-1, keepdims=True)
            e = jnp.exp2(s - peak).astype(bf16)
            o = nn(e, values[:ext, :])
            total = o[:, HEAD:]
            low = peak + jnp.log2(total)
            o = (o[:, :HEAD] / total).astype(bf16)
            att_ref[q_at, cols] = jnp.concatenate([o[h * 128 : (h + 1) * 128] for h in range(GROUP)], axis=1)
            for h in range(GROUP):
                lse = jnp.where(lane == first + h, low[h * 128 : (h + 1) * 128], lse)
        lse_ref[q_at, :] = lse


def attention_forward(lengths, qkv):
    rows, wide = qkv.shape
    model = wide - 2 * HEAD
    return call(
        attention_forward_kernel,
        [shape((rows, model), bf16), shape((rows, HEAD), f32)],
        (lengths, qkv),
        4 * rows * rows * model,
        rows * rows * 4,
        [pltpu.VMEM((rows, 2 * HEAD), bf16), pltpu.VMEM((rows, 2 * HEAD), bf16)],
        VMEM_MIB,
        "attention_forward",
        [SM, VM],
    )


def branch_kernel(sizes, orders, me_ref, x_ref, att_ref, gains_ref, *refs):
    *pieces, wo_ref, hidden_ref, nt_ref = refs

    @pl.when(pl.program_id(0) == 0)
    def _():
        assemble(sizes, me_ref, orders, pieces, wo_ref)

    hidden_ref[...] = x_ref[...].astype(f32) + nn(att_ref[...], wo_ref[...])

    @pl.loop(0, x_ref.shape[0] // 128, unroll=True)
    def _(t):
        at = pl.ds(pl.multiple_of(t * 128, 128), 128)
        nt_ref[at, :] = norm_tile(hidden_ref[at, :], gains_ref[1:2, :]).astype(bf16)


def held(a):
    return pl.BlockSpec(a.shape, lambda i: (0, 0), pipeline_mode=pl.Buffered(1))


def branch(sizes, orders, me, x, att, gains, pieces):
    rows, model = x.shape
    tile = rows // 4
    wo = shape((model, model), bf16)
    strip = pl.BlockSpec((tile, model), lambda i: (i, 0))
    return call(
        functools.partial(branch_kernel, sizes, orders),
        [wo, shape((rows, model), f32), shape((rows, model), bf16)],
        (me, x, att, gains, *pieces),
        2 * rows * model * model,
        0,
        (),
        VMEM_MIB,
        "branch",
        [SM, strip, strip, held(gains), *map(held, pieces)],
        grid=(rows // tile,),
        out_specs=[held(wo), strip, strip],
    )


def gelu_both(v):
    v2 = v * v
    t = jnp.tanh(v * (GELU_A + GELU_B * v2))
    h = 0.5 + 0.5 * t
    a = v * h
    return a, h + (a - a * h) * ((2 * GELU_A) + (6 * GELU_B) * v2)


def ffn_kernel(sizes, order, chunk, joined, me_ref, *refs):
    count, lines = seconds(sizes, order), firsts(sizes, order)
    take = lambda n: [refs.pop(0) for _ in range(n)]
    refs = list(refs)
    near, ins = take(4), take(count)
    take(joined)
    seen, whole, outs = take(4), take(2), take(lines)
    pieces = take(count)
    acts, (up_ref, down_ref), (gu, gd), staged = take(4), take(2), take(2), take(lines)
    in_sem, out_sem = refs
    part, model = down_ref.shape
    shard = part // math.prod(sizes)
    share = slice(chunk * part, (chunk + 1) * part)
    seen = [a.at[:, share] for a in seen]
    whole = [whole[0].at[:, share], whole[1].at[share, :]]
    tile = min(512, part)

    loads = [pltpu.make_async_copy(a, b, in_sem.at[n]) for n, (a, b) in enumerate(zip(ins, pieces))]
    for load in loads:
        load.start()
    started = []

    def store(src, dst):
        copy = pltpu.make_async_copy(src, dst, out_sem.at[len(started)])
        copy.start()
        started.append(copy)

    for load in loads:
        load.wait()
    for place, (first, second) in blocks_of(sizes, order):
        x, f = chip_at(sizes, order, me_ref, *place, -1)
        row = (first * sizes[1] + place[2]) * shard
        at = slice(row, row + shard)
        for core in range(2):
            up_ref[row_of(sizes, x, f, core, shard), :] = pieces[second][at, core * part : (core + 1) * part]
        down_ref[half_row_of(sizes, x, f, shard), :] = pieces[second][at, 2 * part :]

    nt_o, nt_p, dy_o, dy_p = near
    act_o, act_p, gi_o, gi_p = acts
    tiles = [slice(j * tile, (j + 1) * tile) for j in range(part // tile)]
    for j, cols in enumerate(tiles):
        for own, (n_ref, y_ref, a_ref, i_ref) in enumerate(((nt_o, dy_o, act_o, gi_o), (nt_p, dy_p, act_p, gi_p))):
            inner = nn(n_ref[...], up_ref[:, cols])
            ga = nt(y_ref[...], down_ref[cols, :])
            a, slope = gelu_both(inner)
            a_ref[:, cols] = a.astype(bf16)
            i_ref[:, cols] = (ga * slope).astype(bf16)
            if j == len(tiles) - 1:
                store(a_ref, seen[own])
                store(i_ref, seen[2 + own])
    store(up_ref, whole[0])
    store(down_ref, whole[1])
    for cols in tiles:
        gu[:, cols] = (tn(nt_o[...], gi_o[:, cols]) + tn(nt_p[...], gi_p[:, cols])).astype(bf16)
    for cols in tiles:
        gd[cols, :] = (tn(act_o[:, cols], dy_o[...]) + tn(act_p[:, cols], dy_p[...])).astype(bf16)

    for line in reversed(range(lines)):
        for place, (first, second) in blocks_of(sizes, order):
            if first != line:
                continue
            x, f = chip_at(sizes, order, me_ref, *place, 1)
            row = (second * sizes[1] + place[2]) * shard
            at = slice(row, row + shard)
            for core in range(2):
                staged[line][at, core * part : (core + 1) * part] = gu[row_of(sizes, x, f, core, shard), :]
            staged[line][at, 2 * part :] = gd[half_row_of(sizes, x, f, shard), :]
        store(staged[line], outs[line])
    for copy in started:
        copy.wait()


def ffn(sizes, order, chunk, chunks, me, nt_o, nt_p, dy_o, dy_p, pieces, joint):
    rows, model = nt_o.shape
    part = model // 2
    up, down = shape((model, part), bf16), shape((part, model), bf16)
    lines = firsts(sizes, order)
    grads = [shape((part // lines, 2 * model), bf16)] * lines
    ins = (nt_o, nt_p, dy_o, dy_p, *pieces, *joint)
    seen = [shape((rows, part), bf16)] * 4
    outs = [shape((rows, chunks * part), bf16)] * 4
    outs += [shape((model, chunks * part), bf16), shape((chunks * part, model), bf16), *grads]
    far = pl.BlockSpec(memory_space=pltpu.HBM)
    outs = call(
        functools.partial(ffn_kernel, sizes, order, chunk, len(joint)),
        outs,
        (me, *ins),
        16 * rows * model * part,
        2 * rows * part,
        [pltpu.VMEM(a.shape, bf16) for a in (*pieces, *seen, up, down, up, down, *grads)]
        + [pltpu.SemaphoreType.DMA((len(pieces),)), pltpu.SemaphoreType.DMA((len(outs),))],
        FFN_MIB,
        "ffn",
        [SM] + [NEAR] * 4 + [far] * (len(pieces) + len(joint)),
        out_specs=[far] * len(outs),
        input_output_aliases={5 + len(pieces) + n: n for n in range(len(joint))},
    )
    return outs[:6], outs[6:]


def hidden_backward_kernel(gi_ref, up_ref, gn_ref):
    gn_ref[...] = nt(gi_ref[...], up_ref[...]).astype(bf16)


def hidden_backward(gi, up):
    rows, inner = gi.shape
    model = up.shape[0]
    tile = rows // 4
    return call(
        hidden_backward_kernel,
        [shape((rows, model), bf16)],
        (gi, up),
        2 * rows * inner * model,
        0,
        (),
        VMEM_MIB,
        "hidden_backward",
        [pl.BlockSpec((tile, inner), lambda g: (g, 0)), held(up)],
        grid=(rows // tile,),
        out_specs=[pl.BlockSpec((tile, model), lambda g: (g, 0))],
    )[0]


def down_kernel(a_ref, d_ref, *refs):
    *more, out_ref = refs
    total = nn(a_ref[...], d_ref[...])
    for m in more:
        total = total + m[...].astype(f32)
    out_ref[...] = total.astype(bf16)


def down(act, weight, more):
    rows, inner = act.shape
    model = weight.shape[1]
    tile = rows // 4
    strip = pl.BlockSpec((tile, model), lambda g: (g, 0))
    return call(
        down_kernel,
        [shape((rows, model), bf16)],
        (act, weight, *more),
        2 * rows * inner * model,
        0,
        (),
        VMEM_MIB,
        "down",
        [pl.BlockSpec((tile, inner), lambda g: (g, 0)), held(weight)] + [strip] * len(more),
        grid=(rows // tile,),
        out_specs=[strip],
    )[0]


def branch_backward_kernel(sizes, orders, me_ref, hidden_ref, gn_ref, dy_ref, att_ref, gains_ref, wo_ref, gi_ref, up_ref, *refs):
    gh_ref, gatt_ref, gg_ref, *halves, gn, gb, gwo, low = refs
    step = pl.program_id(0)
    rows = hidden_ref.shape[0]

    @pl.when(step == 0)
    def _():
        gg_ref[...] = jnp.zeros_like(gg_ref)
        gwo[...] = jnp.zeros_like(gwo)

    gn[...] = gn_ref[...].astype(f32) + nt(gi_ref[...], up_ref[...])

    @pl.loop(0, rows // 64, unroll=True)
    def _(t):
        at = pl.ds(pl.multiple_of(t * 64, 64), 64)
        h, n = hidden_ref[at, :], gn[at, :]
        r = lax.rsqrt(jnp.mean(h * h, axis=-1, keepdims=True) + EPS)
        z = h * r
        gg_ref[1:2, :] += jnp.sum(n * z, axis=0, keepdims=True)
        g = n * gains_ref[1:2, :]
        gh = dy_ref[at, :].astype(f32) + r * (g - z * jnp.mean(g * z, axis=-1, keepdims=True))
        gh_ref[at, :] = gh
        gb[at, :] = gh.astype(bf16)

    gatt_ref[...] = nt(gb[...], wo_ref[...]).astype(bf16)
    gwo[...] += tn(att_ref[...], gb[...])

    @pl.when(step == pl.num_programs(0) - 1)
    def _():
        low[...] = gwo[...].astype(bf16)
        hand_out(sizes, me_ref, orders, low, halves)


def branch_backward(sizes, orders, me, hidden, gn, dy, att, gains, wo, gi, up):
    rows, model = hidden.shape
    inner = gi.shape[1]
    tile = rows // 4
    strip = pl.BlockSpec((tile, model), lambda i: (i, 0))
    gg = shape((8, model), f32)
    halves = [shape((model // 2, model // len(orders)), bf16)] * (2 * len(orders))
    return call(
        functools.partial(branch_backward_kernel, sizes, orders),
        [shape((rows, model), f32), shape((rows, model), bf16), gg, *halves],
        (me, hidden, gn, dy, att, gains, wo, gi, up),
        4 * rows * model * model + 2 * rows * inner * model,
        0,
        [
            pltpu.VMEM((tile, model), f32),
            pltpu.VMEM((tile, model), bf16),
            pltpu.VMEM((model, model), f32),
            pltpu.VMEM((model, model), bf16),
        ],
        VMEM_MIB,
        "branch_backward",
        [SM, strip, strip, strip, strip, held(gains), held(wo)]
        + [pl.BlockSpec((tile, inner), lambda i: (i, 0)), held(up)],
        grid=(rows // tile,),
        out_specs=[strip, strip, held(gg), *map(held, halves)],
    )


def attention_backward_kernel(
    len_ref, qkv_ref, ga_ref, att_ref, lse_ref, g_ref, keys, values, probs, gscores, dk, dv
):
    rows, wide = qkv_ref.shape
    heads = (wide - 2 * HEAD) // HEAD
    key_at = heads * HEAD
    dk[...] = jnp.zeros_like(dk)
    dv[...] = jnp.zeros_like(dv)
    marked(len_ref, qkv_ref, keys, values)

    for i in range(rows // 128):
        ext = (i + 1) * 128
        q_at = slice(i * 128, ext)
        marks = query_marks(len_ref, i * 128)
        bias = block_bias(len_ref, i * 128)
        for first in range(0, heads, GROUP):
            cols = slice(first * HEAD, (first + GROUP) * HEAD)
            q = stack(qkv_ref[q_at, cols], GROUP)
            ga = stack(ga_ref[q_at, cols], GROUP)
            q_more, ga_more = [], []
            for h in range(first, first + GROUP):
                at = slice(h * HEAD, (h + 1) * HEAD)
                q_more.append(at_lanes(marks, MARKS, split3(-lse_ref[q_at, h : h + 1])).astype(bf16))
                delta = jnp.sum(ga_ref[q_at, at].astype(f32) * att_ref[q_at, at].astype(f32), axis=-1, keepdims=True)
                ga_more.append(at_lanes(jnp.zeros((128, HEAD), f32), 0, split3(-delta)).astype(bf16))
            s = nt(jnp.concatenate([q, jnp.concatenate(q_more, axis=0)], axis=1), keys[:ext, :])
            gp = nt(jnp.concatenate([ga, jnp.concatenate(ga_more, axis=0)], axis=1), values[:ext, :])
            last = s[:, ext - 128 :] + jnp.concatenate([bias] * GROUP, axis=0)
            s = jnp.concatenate([s[:, : ext - 128], last], axis=1) if i else last
            p = jnp.exp2(s)
            out = slice(first * 128, (first + GROUP) * 128)
            probs[out, :ext] = p.astype(bf16)
            gscores[out, :ext] = (p * gp).astype(bf16)
        dv[:ext, :] += tn(probs[:, :ext], stack(ga_ref[q_at, :], heads))
        dk[:ext, :] += tn(gscores[:, :ext], stack(qkv_ref[q_at, :key_at], heads))
        gq = (nn(gscores[:, :ext], keys[:ext, :HEAD]) * SCORE_SCALE).astype(bf16)
        g_ref[q_at, :key_at] = jnp.concatenate([gq[h * 128 : (h + 1) * 128] for h in range(heads)], axis=1)

    g_ref[:, key_at : key_at + HEAD] = (dk[...] * (1.0 / LOG2E)).astype(bf16)
    g_ref[:, key_at + HEAD :] = dv[...].astype(bf16)


def attention_backward(lengths, qkv, ga, att, lse):
    rows, wide = qkv.shape
    model = ga.shape[1]
    return call(
        attention_backward_kernel,
        [shape(qkv.shape, bf16)],
        (lengths, qkv, ga, att, lse),
        10 * rows * rows * model,
        rows * rows * 4,
        [
            pltpu.VMEM((rows, 2 * HEAD), bf16),
            pltpu.VMEM((rows, 2 * HEAD), bf16),
            pltpu.VMEM((model, rows), bf16),
            pltpu.VMEM((model, rows), bf16),
            pltpu.VMEM((rows, HEAD), f32),
            pltpu.VMEM((rows, HEAD), f32),
        ],
        VMEM_MIB,
        "attention_backward",
        [SM] + [VM] * 4,
    )[0]


def projection_grads_kernel(sizes, orders, me_ref, x_ref, g_ref, w_ref, gains_ref, gg_ref, *refs):
    *halves, normed, gw = refs
    rows, model = x_ref.shape
    wide = g_ref.shape[1]

    @pl.loop(0, rows // 128, unroll=True)
    def _(t):
        at = pl.ds(pl.multiple_of(t * 128, 128), 128)
        normed[at, :] = norm_tile(x_ref[at, :].astype(f32), gains_ref[0:1, :]).astype(bf16)

    dots = jnp.zeros((model, HEAD), f32)
    for j in range(wide // 256):
        at = slice(j * 256, (j + 1) * 256)
        v = tn(normed[...], g_ref[:, at])
        gw[:, at] = v.astype(bf16)
        v = v * w_ref[:, at].astype(f32)
        dots = dots + (v[:, :HEAD] + v[:, HEAD:])
    one = jnp.sum(dots, axis=-1, keepdims=True) / w_ref[:, wide : wide + 1].astype(f32)
    two = jnp.concatenate([gg_ref[...], jnp.zeros((HEAD - 8, model), f32)], axis=0).T
    lane = lax.broadcasted_iota(jnp.int32, (model, HEAD), 1)
    gw[:, wide : wide + HEAD] = jnp.where(lane == 0, one, two).astype(bf16)
    hand_out(sizes, me_ref, orders, gw, halves)


def projection_grads(sizes, orders, widths, me, x, g, w, gains, gg):
    rows, model = x.shape
    halves = [shape((w.shape[0] // 2, width), bf16) for width in widths for _ in range(2)]
    return call(
        functools.partial(projection_grads_kernel, sizes, orders),
        halves,
        (me, x, g, w, gains, gg),
        2 * rows * model * g.shape[1],
        0,
        [pltpu.VMEM((rows, model), bf16), pltpu.VMEM(w.shape, bf16)],
        VMEM_MIB,
        "projection_grads",
        [SM] + [VM] * 5,
    )


def input_backward_kernel(x_ref, g_ref, gh_ref, w_ref, gains_ref, gx_ref, gn):
    rows = x_ref.shape[0]
    gn[...] = nt(g_ref[...], w_ref[:, : g_ref.shape[1]])

    @pl.loop(0, rows // 64, unroll=True)
    def _(t):
        at = pl.ds(pl.multiple_of(t * 64, 64), 64)
        x = x_ref[at, :].astype(f32)
        r = lax.rsqrt(jnp.mean(x * x, axis=-1, keepdims=True) + EPS)
        z = x * r
        g = gn[at, :] * gains_ref[0:1, :]
        gx_ref[at, :] = (gh_ref[at, :] + r * (g - z * jnp.mean(g * z, axis=-1, keepdims=True))).astype(bf16)


def input_backward(x, g, gh, w, gains):
    rows, model = x.shape
    tile = rows // 4
    strip = lambda a: pl.BlockSpec((tile, a.shape[1]), lambda i: (i, 0))
    return call(
        input_backward_kernel,
        [shape(x.shape, bf16)],
        (x, g, gh, w, gains),
        2 * rows * model * g.shape[1],
        0,
        [pltpu.VMEM((tile, model), f32)],
        VMEM_MIB,
        "input_backward",
        [strip(x), strip(g), strip(gh), held(w), held(gains)],
        grid=(rows // tile,),
        out_specs=[strip(x)],
    )[0]


def after(a, *first):
    return lax.optimization_barrier((a, *first))[0]


def spread(a, axis, n):
    return [a] + [lax.ppermute(a, axis, [(i, (i + s) % n) for i in range(n)]) for s in range(1, n)]


def add(parts):
    total = parts[0].astype(f32)
    for p in parts[1:]:
        total = total + p.astype(f32)
    return total


def send_on(parts, axis, n):
    return [lax.ppermute(parts[s], axis, [(i, (i + s) % n) for i in range(n)]) for s in range(1, n)]


def cut(a, s, n):
    rows = a.shape[0] // n
    return a[s * rows : (s + 1) * rows]


def cut_columns(a, s, n):
    columns = a.shape[1] // n
    return a[:, s * columns : (s + 1) * columns]


class Hops:
    def __init__(self, sizes, order):
        x, b = ("x", sizes[0]), ("f2", sizes[2])
        self.axes = (x, b) if order[0] else (b, x)

    def gather_one(self, block):
        self.lines = spread(block, *self.axes[0])
        return self.lines[1:]

    def gather_two(self):
        self.pieces = spread(jnp.concatenate(self.lines, axis=0), *self.axes[1])
        return self.pieces

    def reduce_one(self, parts):
        self.got = [parts[0], *send_on(parts, *self.axes[0])]

    def hold(self, *first):
        self.got[1:] = [after(p, *first) for p in self.got[1:]]

    def reduce_two(self):
        n = self.axes[1][1]
        parts = [add([cut(p, s, n) for p in self.got]).astype(bf16) for s in range(n)]
        self.got = [parts[0], *send_on(parts, *self.axes[1])]
        return parts

    def sum_two(self, n=1):
        return [add([cut(p, s, n) for p in self.got]).astype(bf16) for s in range(n)]


def on_device(
    sizes, tokens, doc_lengths, gain_one, query_weight, key_weight, value_weight, out_weight,
    gain_two, up_weight, down_weight, cotangent,
):
    nx, na, nb = sizes
    fsdp = na * nb
    core = lax.axis_index("core")
    me = jnp.stack([lax.axis_index(a) for a in ("x", "f1", "f2", "core")]).astype(jnp.int32)
    swap = lambda a: lax.ppermute(a, "core", [(0, 1), (1, 0)])
    rows, model = tokens.shape
    shard = query_weight.shape[0]
    ff = up_weight.shape[1]
    chunks = down_weight.shape[0] // shard
    part = ff // (2 * chunks)
    wide = 2 * model
    x_then, b_then = (True, True), (False, True)
    by_index = [(c % 2 == 0, False) for c in range(chunks)]

    lane = lax.broadcasted_iota(jnp.int32, (shard, HEAD), 1)
    gain_block = jnp.where(lane == 0, gain_one[:, None], jnp.where(lane == 1, gain_two[:, None], jnp.zeros((), bf16)))
    w_rows = jnp.concatenate([query_weight, key_weight, value_weight, gain_block], axis=1)
    columns = w_rows.shape[1]
    first_share = columns // 256 * HEAD
    w_orders, w_widths = (x_then, b_then), (first_share, columns - first_share)
    w_along = spread(w_rows, "f1", na)

    up = up_weight.reshape(shard, nx, 2, fsdp, chunks, shard).transpose(2, 0, 4, 1, 3, 5)
    up = up.reshape(2, shard, chunks, part)
    up_keep = jnp.where(core == 0, up[0], up[1])
    up_come = swap(jnp.where(core == 0, up[1], up[0]))
    up_pair = jnp.where(core == 0, jnp.stack([up_keep, up_come], 2), jnp.stack([up_come, up_keep], 2))
    up_pair = up_pair.reshape(shard, chunks, wide // 2)
    down_rows = down_weight.reshape(chunks, shard, model)
    f_along = []
    for first in range(0, chunks, 2):
        mine = [p for c in (first, first + 1) for p in (up_pair[:, c], down_rows[c])]
        mine = jnp.concatenate(mine + ([] if first else [out_weight]), axis=1)
        f_along.append(lax.all_gather(after(mine, *w_along[1:]), "f1", axis=0, tiled=True))

    dy_p = swap(after(cotangent, *w_along[1:]))
    w_block = jnp.concatenate(w_along, axis=0)
    w_hops = [Hops(sizes, order) for order in w_orders]
    lines = w_hops[0].gather_one(w_block[:, :first_share]) + w_hops[1].gather_one(w_block[:, first_share:])
    w_pieces = []
    for h in w_hops:
        p = h.gather_two()
        w_pieces += p + [swap(a) for a in p]
    wo_orders, wo_back = ((True, False), (False, False)), (x_then,)
    hops = [Hops(sizes, order) for order in by_index]
    f_lines = lambda c: hops[c].gather_one(cut_columns(f_along[c // 2], c % 2, 2))

    w, qkv, gains = project(sizes, w_orders, columns, me, tokens, w_pieces)
    f_along[0] = after(f_along[0], qkv)
    wo_block, f_along[0] = f_along[0][:, 2 * wide :], f_along[0][:, : 2 * wide]
    wo_hops = [Hops(sizes, order) for order in wo_orders]
    for n, h in enumerate(wo_hops):
        h.gather_one(cut_columns(wo_block, n, 2))
    lines = [p for c in (0, 1) for p in f_lines(c)]
    att, lse = attention_forward(doc_lengths, after(qkv, dy_p))
    for h in wo_hops:
        h.lines[1:] = [after(p, att) for p in h.lines[1:]]
    wo_pieces = [h.gather_two() for h in wo_hops]
    wo_pieces = [a for p in wo_pieces for a in (*p, *[swap(b) for b in p])]
    for c in (0, 1):
        hops[c].lines[1:] = [after(p, att, *[h.pieces[1] for h in wo_hops]) for p in hops[c].lines[1:]]
    pieces = {c: hops[c].gather_two() for c in (0, 1)}
    wo, hidden, nt_o = branch(sizes, wo_orders, me, tokens, att, gains, wo_pieces)
    nt_o = after(nt_o, *pieces[0], *pieces[1], f_along[1])
    nt_p = swap(nt_o)

    grads, joint = [], []

    def run_ffn(c, *first):
        joint[:], sent = ffn(
            sizes, by_index[c], c, chunks, me, after(nt_o, *first), nt_p, cotangent, dy_p, pieces[c], joint
        )
        grads.append(sent)

    def sum_cores(keep, come, order):
        n = firsts(sizes, order)
        return [add([cut(a, s, n) for a in (keep, come)]).astype(bf16) for s in range(n)]

    f_along[1] = after(f_along[1], nt_p)
    lines = [p for c in (2, 3) for p in f_lines(c)]
    run_ffn(0)
    run_ffn(1, *lines)
    for c in (2, 3):
        hops[c].lines[1:] = [after(p, grads[0][0]) for p in hops[c].lines[1:]]
        pieces[c] = hops[c].gather_two()
    late = [*pieces[2], *pieces[3], grads[1][0]]
    run_ffn(2, *late)
    for c in (0, 1):
        hops[c].reduce_one([after(g, *late) for g in grads[c]])
    run_ffn(3)
    for c in (0, 1):
        hops[c].hold(grads[3][0])
    act_o, act_p, gi_o, gi_p, up, down_whole = joint
    ready = [p for c in (0, 1) for p in hops[c].reduce_two()]
    for c in (2, 3):
        hops[c].reduce_one([after(g, *ready) for g in grads[c]])
    gn_p = hidden_backward(after(gi_p, *ready), up)
    gn_r = swap(gn_p)
    out_p = down(after(act_p, gn_p), down_whole, [])
    last = lambda a: lax.psum_scatter(a, "f1", scatter_dimension=0, tiled=True)
    for c in (0, 1):
        hops[c].hold(out_p)
    pair = jnp.concatenate([hops[c].sum_two()[0] for c in (0, 1)], axis=1)
    sums = [last(pair)]
    gh, gatt, gg, *halves = branch_backward(
        sizes, wo_back, me, hidden, gn_r, cotangent, att, gains, wo, after(gi_o, pair), up
    )
    for c in (2, 3):
        hops[c].hold(gatt)
    ready = [p for c in (2, 3) for p in hops[c].reduce_two()]
    come = swap(after(halves[1], *ready))
    wo_reduce = Hops(sizes, x_then)
    ready = sum_cores(halves[0], come, x_then)
    wo_reduce.reduce_one(ready)
    g = attention_backward(doc_lengths, after(qkv, *ready), gatt, att, lse)
    for h in (hops[2], hops[3], wo_reduce):
        h.hold(g)
    pair = jnp.concatenate([hops[c].sum_two()[0] for c in (2, 3)], axis=1)
    sums.append(last(pair))
    ready = wo_reduce.reduce_two()
    out_r = swap(after(out_p, g))
    halves = projection_grads(sizes, w_orders, w_widths, me, after(tokens, *ready, pair), g, w, gains, gg)
    wo_reduce.hold(halves[0])
    wo_last = wo_reduce.sum_two()[0]
    come = [swap(after(h, wo_last)) for h in halves[1::2]]
    ready = [sum_cores(k, c, o) for k, c, o in zip(halves[0::2], come, w_orders)]
    w_reduce = [Hops(sizes, order) for order in w_orders]
    for h, r in zip(w_reduce, ready):
        h.reduce_one(r)
    ready = [r for rs in ready for r in rs]
    grad_tokens = input_backward(after(tokens, *ready), g, gh, w, gains)
    ready = []
    for h in w_reduce:
        h.hold(grad_tokens)
        ready += h.reduce_two()
    output = down(after(act_o, *ready), down_whole, [hidden, out_r])
    for h in w_reduce:
        h.hold(output)
    w_parts = [jnp.concatenate([*p, cut(wo_last, n, na)], axis=1) for n, p in enumerate(zip(*[h.sum_two(na) for h in w_reduce]))]
    got = send_on(w_parts, "f1", na)

    sums = [after(a, *w_parts) for a in sums]
    sums = jnp.stack([a.reshape(shard, 2, wide) for a in sums], axis=1).reshape(shard, chunks, wide)
    grad_down = sums[:, :, model:].transpose(1, 0, 2).reshape(chunks * shard, model).astype(f32)
    g_up = sums[:, :, :model].reshape(shard, chunks, 2, part)
    keep = jnp.where(core == 0, g_up[:, :, 0], g_up[:, :, 1])
    come = swap(jnp.where(core == 0, g_up[:, :, 1], g_up[:, :, 0]))
    grad_up = jnp.where(core == 0, jnp.stack([keep, come], 0), jnp.stack([come, keep], 0))
    grad_up = grad_up.reshape(2, shard, chunks, nx, fsdp, shard).transpose(1, 3, 0, 4, 2, 5)
    grad_up = grad_up.reshape(shard, ff).astype(f32)
    gw = add([w_parts[0], *got])
    grad_out = gw[:, columns:]

    qw = query_weight.shape[1]
    return (
        output,
        grad_tokens,
        gw[:, qw + 2 * HEAD],
        gw[:, :qw],
        gw[:, qw : qw + HEAD],
        gw[:, qw + HEAD : qw + 2 * HEAD],
        grad_out,
        gw[:, qw + 2 * HEAD + 1],
        grad_up,
        grad_down,
    )


def solution(mesh):
    dp, fsdp = mesh.shape["dp"], mesh.shape["fsdp"]
    sizes = (dp // 2, 4, fsdp // 4)
    names = ("x", "core", "f1", "f2")
    split = Mesh(mesh.devices.reshape(sizes[0], 2, *sizes[1:]), names)
    rows, line = P(names, None), P(names)
    return jax.shard_map(
        functools.partial(on_device, sizes),
        mesh=split,
        in_specs=(rows, rows, line, rows, rows, rows, rows, line, rows, rows, rows),
        out_specs=(rows, rows, line, rows, rows, rows, rows, line, rows, rows),
        check_vma=False,
    )
```
